256 devices in a mesh: dp: 64 (over z, y, x_lo), mp: 4 (over x_hi, core).
Axes of the slice: x: 4 (x_hi: 2, x_lo: 2; x = x_hi * 2 + x_lo), y: 4, z: 8, core: 2. Of those that a mesh axis runs over, the one named last changes fastest.
Arguments:
- tokens: bfloat16 [18432, 5120], P(('dp', 'mp')), may hold values from -24 to 24
- gate_weight: bfloat16 [5120, 8704], P('dp', 'mp'), may hold values from -0.078125 to 0.078125
- grad_hidden: bfloat16 [8192, 8704], P('dp', 'mp'), may hold values from -16 to 16
- counts: int32 [64], P('dp'), may hold values from 1 to 288, 6144 in all
- sampled: int32 [8192], P('dp'), may hold values from 0 to 287
- owner_map: int32 [64], replicated, may hold values from 0 to 63, each once
- input_factor: float32 [4, 1280, 128], P('mp', 'dp'), may hold values from -3 to 3
- grad_factor: float32 [4, 2176, 128], P('mp', 'dp'), may hold values from -3 to 3
Outputs:
- activation: bfloat16 [18432, 8704], P('dp', 'mp')
- input_ema: float32 [4, 1280, 128], P('mp', 'dp')
- grad_ema: float32 [4, 2176, 128], P('mp', 'dp')
The draws below stay inside these ranges and needn't reach their ends.
Inputs may be any that keep to these rules, and one draw needn't show every extreme that they name: The largest count is 288; the sum of the counts differs between draws. `sampled`: positions may lie past their group's count. `owner_map`: each rank once.
All inputs are finite; a program needn't handle non-finite values. No bound on the sum of `counts` on one device may be relied on, other than what follows from the above.
Results may differ from the reference program's by a relative error of at most 0.0014.
Values may be sent and summed in bfloat16 or wider, within the bound.
No kernel may reach another device: no remote copies, remote signals or barrier semaphores. Data moves between devices by JAX's collectives and lax.ppermute only.
A program may use at most 128 MiB of HBM per device.

```python
import math
import jax
import jax.numpy as jnp
import numpy as np
from jax import lax

D = 5120
FF_W = 8704
BLK = 128
TOK_DEV = 288
SAMP = 128
TOKENS = 18432
N_DP = 64
N_MP = 4


def place_ends(values, own_key, least, largest):
    spot = [jax.random.randint(jax.random.fold_in(own_key, axis), (), 0, length) for axis, length in enumerate(values.shape)]
    main_axis = values.shape.index(max(values.shape))
    beside = spot[:main_axis] + [(spot[main_axis] + 1) % values.shape[main_axis]] + spot[main_axis + 1:]
    return values.at[tuple(spot)].set(least).at[tuple(beside)].set(largest)


def spiked(array, key, source, target, blocks, factor):
    owner, partner = [(jnp.arange(array.shape[dim]) // (array.shape[dim] // blocks)).reshape([-1 if axis == dim else 1 for axis in range(array.ndim)]) for dim in (source, target)]
    chosen = jax.random.permutation(key, blocks)[partner]
    strong = (owner == chosen) | (owner == (partner + blocks // 2) % blocks)
    return jnp.where(strong, factor * array, array)


def steps_of(rng, dims, cuts, low, top_value):
    gain, own = 1.0, jax.random.fold_in(rng, 6)
    for axis_at, parts in cuts:
        draws = jnp.exp(jax.random.uniform(jax.random.fold_in(own, axis_at), (parts,), jnp.float32, low / len(cuts), top_value / len(cuts)))
        gain = gain * jnp.repeat(draws, dims[axis_at] // parts).reshape([-1 if axis == axis_at else 1 for axis in range(len(dims))])
    return gain


def length_profile(amount, total, bound, slope):
    weights = [(1 << 20) // math.isqrt(rank ** slope) + 1 for rank in range(2, amount + 1)]
    spare, holding = total - bound - (amount - 1), [1] * (amount - 1)
    while spare > 0:
        candidates = [i for i in range(amount - 1) if holding[i] < bound]
        pool, remaining = sum([weights[i] for i in candidates]), spare
        for i in candidates:
            more = min(bound - holding[i], max(1, remaining * weights[i] // pool), spare)
            holding[i] = holding[i] + more
            spare = spare - more
    return np.array([bound] + holding)


def ragged(own_key, count, total, most, slope):
    if count == 2:
        one = jax.random.randint(own_key, (), max(1, total - most), min(most, total - 1) + 1)
        return jnp.stack([one, total - one])
    lengths = jnp.asarray(length_profile(count, total, most, slope), jnp.int32)
    couples = (count - 1) // 2
    donor, receiver = lengths[1:1 + 2 * couples:2], lengths[2:2 + 2 * couples:2]
    margin = jnp.minimum(donor - 1, most - receiver)
    shifted = jax.random.randint(jax.random.fold_in(own_key, 1), (couples,), 0, 1 << 20) % (margin + 1)
    lengths = lengths.at[1:1 + 2 * couples:2].set(donor - shifted).at[2:2 + 2 * couples:2].set(receiver + shifted)
    return lengths[jax.random.permutation(jax.random.fold_in(own_key, 2), count)]


def noise(own_key, dims, spread, bound, pieces=(), kind=jnp.bfloat16):
    gain = steps_of(own_key, dims, pieces, -0.22, 0.18) if pieces else 1.0
    drawn = jax.random.normal(own_key, dims, jnp.float32) * spread * gain
    return jnp.minimum(jnp.maximum(drawn, -bound), bound).astype(kind)


def heavy_noise(own_key, shape, spread, most, pieces, heavy, kind=jnp.bfloat16):
    result = spread * jax.random.normal(own_key, shape, jnp.float32)
    if pieces:
        result = result * steps_of(own_key, shape, pieces, -0.22, 0.18)
    return jnp.clip(spiked(result, jax.random.fold_in(own_key, 3), *heavy), -most, most).astype(kind)


def setup_inputs(seed: int = 0) -> dict:
    streams_of = jax.random.split(jax.random.key(seed), 9)
    tokens = heavy_noise(streams_of[0], (TOKENS, D), 1.0, 24.0, ((0, 256),), (0, 1, 256, 6.0))
    gate_weight = noise(streams_of[1], (D, FF_W), D ** -0.5, 0.078125, ((0, 64), (1, 4)))
    grad_hidden = heavy_noise(streams_of[2], (N_DP * SAMP, FF_W), 1.0, 16.0, ((0, 64), (1, 4)), (0, 1, 64, 4.0))
    counts = ragged(streams_of[3], N_DP, N_DP * TOK_DEV // 3, TOK_DEV, 2).astype(jnp.int32)
    sampled = place_ends(jax.random.randint(streams_of[4], (N_DP * SAMP,), 0, TOK_DEV), jax.random.fold_in(streams_of[4], 1), 0, TOK_DEV - 1).astype(jnp.int32)
    owner_map = jax.random.permutation(streams_of[5], N_DP).astype(jnp.int32)
    input_factor = noise(streams_of[6], (N_MP, D // N_MP, BLK), 0.5, 3.0, ((0, 4), (1, 64)), jnp.float32)
    grad_factor = noise(streams_of[7], (N_MP, FF_W // N_MP, BLK), 0.5, 3.0, ((0, 4), (1, 64)), jnp.float32)
    return dict(tokens=tokens, gate_weight=gate_weight, grad_hidden=grad_hidden, counts=counts, sampled=sampled, owner_map=owner_map, input_factor=input_factor, grad_factor=grad_factor)


EMA_DECAY = 0.8


def block_grams(matrix_rows, blk_size):
    n_blocks = matrix_rows.shape[1] // blk_size
    wide_rows = matrix_rows.astype(jnp.float32)

    def one_block(index):
        columns = lax.dynamic_slice_in_dim(wide_rows, index * blk_size, blk_size, 1)
        return jnp.dot(columns.T, columns, preferred_element_type=jnp.float32)

    grams = lax.map(one_block, jnp.arange(n_blocks, dtype=jnp.int32))
    return grams.reshape(n_blocks * blk_size, blk_size)


def place_strips(statistic, owner_map, n_regions):
    strip_grid = statistic.reshape(n_regions, N_DP, -1, BLK)
    return jnp.take(strip_grid, owner_map, axis=1).reshape(n_regions, -1, BLK)


def reference(tokens, gate_weight, grad_hidden, counts, sampled, owner_map, input_factor, grad_factor):
    grouped = tokens.reshape(N_DP, TOK_DEV, D)
    is_live = jnp.arange(TOK_DEV, dtype=jnp.int32)[None, :] < counts[:, None]
    weight_wide = gate_weight.astype(jnp.float32)

    def recompute(inputs):
        rows_in, live_rows = inputs
        gate_sums = jnp.dot(rows_in.astype(jnp.float32), weight_wide, preferred_element_type=jnp.float32)
        return jnp.where(live_rows[:, None], jax.nn.silu(gate_sums), 0.0).astype(jnp.bfloat16)

    activation = lax.map(recompute, (grouped, is_live))
    masked = jnp.where(is_live[:, :, None], grouped, jnp.zeros((), jnp.bfloat16)).reshape(TOKENS, D)
    all_tokens = jnp.sum(counts).astype(jnp.float32)
    input_stat = block_grams(masked, BLK) / all_tokens
    sample_rows = sampled.reshape(N_DP, SAMP)
    picked = jax.vmap(lambda table, where_at: jnp.take(table, where_at, axis=0))(activation, sample_rows)
    picked = picked.reshape(N_DP * SAMP, FF_W)
    grad_rows = (grad_hidden.astype(jnp.float32) * picked.astype(jnp.float32)).astype(jnp.bfloat16)
    grad_stat = block_grams(grad_rows, BLK) / jnp.float32(N_DP * SAMP)
    input_ema = EMA_DECAY * input_factor + (1.0 - EMA_DECAY) * place_strips(input_stat, owner_map, N_MP)
    grad_ema = EMA_DECAY * grad_factor + (1.0 - EMA_DECAY) * place_strips(grad_stat, owner_map, N_MP)
    return activation.reshape(TOKENS, FF_W), input_ema, grad_ema
```

```python
import jax
import jax.numpy as jnp
from jax import lax
from jax.sharding import Mesh, PartitionSpec as P

EMA_DECAY = 0.8
NZ, NY = 8, 4
DP = ("z", "y", "xl")
MP = ("xh", "c")


def swap(x, axis):
    return lax.ppermute(x, axis, [(0, 1), (1, 0)])


def block_grams(rows, blk):
    stacked = rows.reshape(rows.shape[0], -1, blk)
    grams = jnp.einsum("tkb,tkc->kbc", stacked, stacked, preferred_element_type=jnp.float32)
    return grams.reshape(-1, blk)


def scatter_strips(statistic, owner_map, send_type):
    blk = statistic.shape[-1]
    n_dp = owner_map.shape[0]
    strips = statistic.astype(send_type).reshape(n_dp, -1, blk)
    height = strips.shape[1]
    slots = jnp.take(strips, owner_map, axis=0).reshape(NZ, NY, 2, height, blk)
    got = lax.all_to_all(slots, "y", 1, 1, tiled=False)
    part = jnp.sum(got.astype(jnp.float32), axis=1)
    got = lax.all_to_all(part, "xl", 1, 1, tiled=False)
    part = jnp.sum(got, axis=1)
    got = lax.all_to_all(part, "z", 0, 0, tiled=False)
    return jnp.sum(got, axis=0)


def local(tokens, gate_weight, grad_hidden, counts, sampled, owner_map, input_factor, grad_factor):
    blk = input_factor.shape[2]
    n_dp = owner_map.shape[0]
    xl = lax.axis_index("xl")
    c = lax.axis_index("c")
    mp = lax.axis_index("xh") * 2 + c
    panel = gate_weight.shape[1]
    half_blocks = (panel // blk + 1) // 2
    width = half_blocks * blk
    step = panel - width

    mine = lax.dynamic_slice_in_dim(gate_weight, xl * step, width, 1)
    theirs = lax.dynamic_slice_in_dim(gate_weight, (1 - xl) * step, width, 1)
    got = swap(theirs, "xl")
    first = jnp.where(xl == 0, mine, got)
    second = jnp.where(xl == 0, got, mine)
    shard = jnp.concatenate([first, second], axis=0)
    weight = lax.all_gather(shard, ("z", "y"), axis=0, tiled=True)

    all_counts = lax.all_gather(counts, DP, axis=0, tiled=True)
    all_tokens = jnp.sum(all_counts).astype(jnp.float32)
    other_count = swap(counts, "xl")[0]

    group = lax.all_gather(tokens, MP, axis=0, tiled=True)
    tok_dev = group.shape[0]
    part = lax.dynamic_slice_in_dim(group, c * (tok_dev // 2), tok_dev // 2, 0)
    other_part = swap(part, "xl")
    other_rest = swap(other_part, "c")
    other = jnp.where(
        c == 0,
        jnp.concatenate([other_part, other_rest], axis=0),
        jnp.concatenate([other_rest, other_part], axis=0),
    )
    slot = lax.iota(jnp.int32, tok_dev)
    live_own = slot < counts[0]
    live_other = slot < other_count

    region = tokens.shape[1] // (2 * 2)
    own_columns = lax.dynamic_slice_in_dim(group, mp * region, region, 1)
    own_columns = jnp.where(live_own[:, None], own_columns, jnp.zeros((), jnp.bfloat16))
    input_stat = scatter_strips(block_grams(own_columns, blk), owner_map, jnp.float32)
    input_ema = EMA_DECAY * input_factor + (1.0 - EMA_DECAY) * (input_stat / all_tokens).reshape(
        input_factor.shape
    )

    def gate(rows, live):
        sums = jnp.dot(rows, weight, preferred_element_type=jnp.float32)
        return jnp.where(live[:, None], jax.nn.silu(sums), 0.0).astype(jnp.bfloat16)

    act_other = gate(other, live_other)
    act_own = gate(group, live_own)
    away = lax.dynamic_slice_in_dim(act_other, xl * (width - step), step, 1)
    back = swap(away, "xl")
    activation = jnp.where(
        xl == 0,
        jnp.concatenate([act_own, back], axis=1),
        jnp.concatenate([back, act_own], axis=1),
    )

    pick = (sampled[:, None] == slot[None, :]).astype(jnp.bfloat16)
    picked = jnp.dot(pick, activation, preferred_element_type=jnp.float32)
    grad_rows = (grad_hidden.astype(jnp.float32) * picked).astype(jnp.bfloat16)
    grad_stat = scatter_strips(block_grams(grad_rows, blk), owner_map, jnp.float32)
    sample_total = jnp.float32(grad_hidden.shape[0] * n_dp)
    grad_ema = EMA_DECAY * grad_factor + (1.0 - EMA_DECAY) * (grad_stat / sample_total).reshape(
        grad_factor.shape
    )
    return (activation, input_ema, grad_ema)


def solution(mesh):
    fine = Mesh(mesh.devices.reshape(NZ, NY, 2, 2, 2), ("z", "y", "xl", "xh", "c"))
    in_specs = (
        P(DP + MP, None),
        P(DP, MP),
        P(DP, MP),
        P(DP),
        P(DP),
        P(),
        P(MP, DP, None),
        P(MP, DP, None),
    )
    out_specs = (P(DP, MP), P(MP, DP, None), P(MP, DP, None))
    return jax.shard_map(local, mesh=fine, in_specs=in_specs, out_specs=out_specs, check_vma=False)
```

```python
import jax
import jax.numpy as jnp
from jax import lax
from jax.sharding import Mesh, PartitionSpec as P

EMA_DECAY = 0.8
NZ, NY = 8, 4
DP = ("z", "y", "xl")
MP = ("xh", "c")


def swap(x, axis):
    return lax.ppermute(x, axis, [(0, 1), (1, 0)])


def shift(x, axis, n, by):
    return lax.ppermute(x, axis, [(i, (i + by) % n) for i in range(n)])


def put(buf, piece, index, dim):
    return lax.dynamic_update_slice_in_dim(buf, jnp.expand_dims(piece, dim), index, dim)


def ring_gather(x, axis, n, dim):
    me = lax.axis_index(axis)
    shape = x.shape[:dim] + (n,) + x.shape[dim:]
    buf = put(jnp.zeros(shape, x.dtype), x, me, dim)
    half = x.shape[0] // 2
    up, down = x, x
    for k in range(1, n // 2):
        up, down = shift(up, axis, n, 1), shift(down, axis, n, -1)
        buf = put(buf, up, lax.rem(me - k + n, n), dim)
        buf = put(buf, down, lax.rem(me + k, n), dim)
    last = jnp.concatenate([shift(up[:half], axis, n, 1), shift(down[half:], axis, n, -1)], axis=0)
    return put(buf, last, lax.rem(me + n // 2, n), dim)


def block_grams(rows, blk):
    stacked = rows.reshape(rows.shape[0], -1, blk)
    return jnp.einsum("tkb,tkc->kbc", stacked, stacked, preferred_element_type=jnp.float32)


def scatter_strips(slots):
    xl = lax.axis_index("xl")
    got = lax.all_to_all(slots, "y", 1, 1, tiled=False)
    part = jnp.sum(got.astype(jnp.float32), axis=1)
    got = lax.all_to_all(part, "z", 0, 0, tiled=False)
    part = jnp.sum(got, axis=0)
    here = lax.dynamic_index_in_dim(part, xl, 0, keepdims=False)
    there = lax.dynamic_index_in_dim(part, 1 - xl, 0, keepdims=False)
    return here + swap(there, "xl")


def local(tokens, gate_weight, grad_hidden, counts, sampled, owner_map, input_factor, grad_factor):
    blk = input_factor.shape[2]
    n_dp = owner_map.shape[0]
    feat = tokens.shape[1]
    xl = lax.axis_index("xl")
    xh = lax.axis_index("xh")
    c = lax.axis_index("c")
    mp = xh * 2 + c
    panel = gate_weight.shape[1]
    half_blocks = (panel // blk + 1) // 2
    width = half_blocks * blk
    step = panel - width
    cut = (half_blocks + 1) // 2 * blk

    mine = lax.dynamic_slice_in_dim(gate_weight, xl * step, width, 1)
    theirs = lax.dynamic_slice_in_dim(gate_weight, (1 - xl) * step, width, 1)
    got = swap(theirs, "xl")
    shard = jnp.where(
        xl == 0, jnp.concatenate([mine, got], axis=0), jnp.concatenate([got, mine], axis=0)
    )
    part_a = ring_gather(shard[:, :cut], "z", NZ, 0)
    part_a = ring_gather(part_a, "y", NY, 1)
    part_b = ring_gather(shard[:, cut:], "y", NY, 0)
    part_b = ring_gather(part_b.reshape(-1, width - cut), "z", NZ, 0)
    weight_a = part_a.reshape(feat, cut)
    weight_b = part_b.reshape(feat, width - cut)

    from_xh = swap(tokens, "xh")
    from_xl = swap(tokens, "xl")
    from_both = lax.ppermute(tokens, ("xl", "xh"), [(0, 3), (1, 2), (2, 1), (3, 0)])
    same = jnp.where(
        xh == 0,
        jnp.stack([tokens, from_xh, from_xl, from_both]),
        jnp.stack([from_xh, tokens, from_both, from_xl]),
    )
    cross = swap(same, "c")
    rows = jnp.where(c == 0, jnp.stack([same, cross], axis=1), jnp.stack([cross, same], axis=1))
    tok_dev = rows.shape[2] * 4
    rows = rows.reshape(2, tok_dev, feat)
    group = rows[0]

    scalars = jnp.concatenate([counts, sampled])
    other_scalars = swap(scalars, "xl")
    slot = lax.iota(jnp.int32, tok_dev)
    live_own = slot < counts[0]
    live_other = slot < other_scalars[0]
    live = jnp.concatenate([live_own, live_other])

    region = feat // 4
    own_columns = lax.dynamic_slice_in_dim(group, mp * region, region, 1)
    own_columns = jnp.where(live_own[:, None], own_columns, jnp.zeros((), jnp.bfloat16))
    strips = jnp.take(block_grams(own_columns, blk).reshape(n_dp, -1, blk), owner_map, axis=0)
    height = strips.shape[1]
    count_row = jnp.broadcast_to(counts[0].astype(jnp.float32), (n_dp, 1, blk))
    slots = jnp.concatenate([strips, count_row], axis=1).reshape(NZ, NY, 2, height + 1, blk)
    summed = scatter_strips(slots)
    input_stat = summed[:height] / summed[height:]
    input_ema = EMA_DECAY * input_factor + (1.0 - EMA_DECAY) * input_stat[None]

    def gate(weight):
        sums = jnp.dot(rows.reshape(2 * tok_dev, feat), weight, preferred_element_type=jnp.float32)
        return jnp.where(live[:, None], jax.nn.silu(sums), 0.0).astype(jnp.bfloat16)

    grad_mine = lax.dynamic_slice_in_dim(grad_hidden, xl * step, width, 1)
    grad_theirs = lax.dynamic_slice_in_dim(grad_hidden, (1 - xl) * step, width, 1)
    grad_got = swap(grad_theirs, "xl")
    pick_own = (sampled[:, None] == slot[None, :]).astype(jnp.bfloat16)
    pick_other = (other_scalars[1:, None] == slot[None, :]).astype(jnp.bfloat16)

    def grams(act, lo, hi):
        own = jnp.dot(pick_own, act[:tok_dev], preferred_element_type=jnp.float32)
        other = jnp.dot(pick_other, act[tok_dev:], preferred_element_type=jnp.float32)
        own = (grad_mine[:, lo:hi].astype(jnp.float32) * own).astype(jnp.bfloat16)
        other = (grad_got[:, lo:hi].astype(jnp.float32) * other).astype(jnp.bfloat16)
        return block_grams(jnp.concatenate([own, other], axis=0), blk)

    act_b = gate(weight_b)
    grams_b = grams(act_b, cut, width)
    act_a = gate(weight_a)
    grams_a = grams(act_a, 0, cut)
    act = jnp.concatenate([act_a, act_b], axis=1)
    gram = jnp.concatenate([grams_a, grams_b], axis=0)

    away = lax.dynamic_slice_in_dim(act[tok_dev:], xl * (width - step), step, 1)
    back = swap(away, "xl")
    activation = jnp.where(
        xl == 0,
        jnp.concatenate([act[:tok_dev], back], axis=1),
        jnp.concatenate([back, act[:tok_dev]], axis=1),
    )

    n_rest = panel // blk - half_blocks
    gram = jnp.where(
        xl == 0,
        jnp.concatenate([gram, jnp.zeros((n_rest, blk, blk), jnp.float32)], axis=0),
        jnp.concatenate([jnp.zeros((half_blocks, blk, blk), jnp.float32), gram[-n_rest:]], axis=0),
    )
    strips = jnp.take(gram.astype(jnp.bfloat16).reshape(n_dp, -1, blk), owner_map, axis=0)
    grad_stat = scatter_strips(strips.reshape(NZ, NY, 2, -1, blk))
    sample_total = jnp.float32(grad_hidden.shape[0] * n_dp)
    grad_ema = EMA_DECAY * grad_factor + (1.0 - EMA_DECAY) * (grad_stat / sample_total)[None]
    return (activation, input_ema, grad_ema)


def solution(mesh):
    fine = Mesh(mesh.devices.reshape(NZ, NY, 2, 2, 2), ("z", "y", "xl", "xh", "c"))
    in_specs = (
        P(DP + MP, None),
        P(DP, MP),
        P(DP, MP),
        P(DP),
        P(DP),
        P(),
        P(MP, DP, None),
        P(MP, DP, None),
    )
    out_specs = (P(DP, MP), P(MP, DP, None), P(MP, DP, None))
    return jax.shard_map(local, mesh=fine, in_specs=in_specs, out_specs=out_specs, check_vma=False)
```

```python
import jax
import jax.numpy as jnp
from jax import lax
from jax.sharding import Mesh, PartitionSpec as P

EMA_DECAY = 0.8
NZ, NY = 8, 4
DP = ("z", "y", "xl")
MP = ("xh", "c")


def swap(x, axis):
    return lax.ppermute(x, axis, [(0, 1), (1, 0)])


def after(x, earlier):
    return lax.optimization_barrier((x, earlier))[0]


def shift(x, axis, n, by):
    return lax.ppermute(x, axis, [(i, (i + by) % n) for i in range(n)])


def put(buf, piece, index, dim):
    return lax.dynamic_update_slice_in_dim(buf, jnp.expand_dims(piece, dim), index, dim)


def place(buf, blocks, dim):
    for at, block in blocks:
        buf = put(buf, block, lax.rem(at, buf.shape[dim]), dim)
    return buf


def both_ways(pair, axis, n):
    return shift(pair[0], axis, n, 1), shift(pair[1], axis, n, -1)


def halves(pair):
    rows = pair[0].shape[0] // 2
    return pair[0][:rows], pair[1][rows:]


def block_grams(rows, blk):
    stacked = rows.reshape(rows.shape[0], -1, blk)
    return jnp.einsum("tkb,tkc->kbc", stacked, stacked, preferred_element_type=jnp.float32)


def pair_strips(strips, owner_map):
    xl = lax.axis_index("xl")
    slots = jnp.take(strips, owner_map, axis=0, mode="clip")
    slots = slots.reshape((NZ * NY, 2) + strips.shape[1:])
    here = lax.dynamic_index_in_dim(slots, xl, 1, keepdims=False)
    there = lax.dynamic_index_in_dim(slots, 1 - xl, 1, keepdims=False)
    return here, there


def scatter_slots(slots):
    got = lax.all_to_all(slots, ("z", "y"), 0, 0, tiled=False)
    return jnp.sum(got.astype(jnp.float32), axis=0)


def local(tokens, gate_weight, grad_hidden, counts, sampled, owner_map, input_factor, grad_factor):
    blk = input_factor.shape[2]
    n_dp = owner_map.shape[0]
    feat = tokens.shape[1]
    xl = lax.axis_index("xl")
    xh = lax.axis_index("xh")
    c = lax.axis_index("c")
    mp = xh * 2 + c
    panel = gate_weight.shape[1]
    half_blocks = (panel // blk + 1) // 2
    width = half_blocks * blk
    step = panel - width
    cut = half_blocks // 2 * blk
    z, y = lax.axis_index("z"), lax.axis_index("y")
    mine = lax.dynamic_slice_in_dim(gate_weight, xl * step, width, 1)
    theirs = lax.dynamic_slice_in_dim(gate_weight, (1 - xl) * step, width, 1)
    got = swap(theirs, "xl")
    shard = jnp.where(
        xl == 0, jnp.concatenate([mine, got], axis=0), jnp.concatenate([got, mine], axis=0)
    )
    def join(first, second, index, dim):
        return jnp.where(
            index == 0, jnp.stack([first, second], axis=dim), jnp.stack([second, first], axis=dim)
        )

    tok_dev = 4 * tokens.shape[0]
    slot = lax.iota(jnp.int32, tok_dev)
    scalars = swap(jnp.concatenate([counts, sampled]), "xl")

    a0, b0 = shard[:, :cut], shard[:, cut:]
    a1 = both_ways((a0, a0), "z", NZ)
    b_side = [shift(b0, "y", NY, k) for k in range(1, NY)]
    from_xh = swap(after(tokens, got), "xh")

    inner = jnp.zeros((NY,) + b0.shape, b0.dtype)
    inner = place(inner, [(y, b0)] + [(y - k + NY, b_side[k - 1]) for k in range(1, NY)], 0)
    inner, a1 = lax.optimization_barrier((inner.reshape(-1, b0.shape[1]), a1))
    b1 = both_ways((inner, inner), "z", NZ)
    a2 = both_ways(a1, "z", NZ)
    a3 = both_ways(a2, "z", NZ)

    a3, b1, from_xh, scalars = lax.optimization_barrier((a3, b1, from_xh, scalars))
    a4 = both_ways(halves(a3), "z", NZ)
    b2 = both_ways(b1, "z", NZ)
    same = join(tokens, from_xh, xh, 0)
    cross = swap(same, "c")

    a4, cross = lax.optimization_barrier((a4, cross))
    outer = jnp.zeros((NZ,) + a0.shape, a0.dtype)
    outer = place(
        outer,
        [(z, a0), (z + NZ - 1, a1[0]), (z + 1, a1[1]), (z + NZ - 2, a2[0]), (z + 2, a2[1])]
        + [(z + NZ - 3, a3[0]), (z + 3, a3[1]), (z + 4, jnp.concatenate(a4, axis=0))],
        0,
    )
    y1 = both_ways((outer, outer), "y", NY)
    other_first = swap(after(tokens, cross), "xl")
    other_second = lax.ppermute(
        after(tokens, cross), ("xl", "xh"), [(0, 3), (1, 2), (2, 1), (3, 0)]
    )
    group = join(same, cross, c, 1).reshape(tok_dev, feat)
    live_own = slot < counts[0]
    live_other = slot < scalars[0]
    live = jnp.concatenate([live_own, live_other])

    region = feat // 4
    own_columns = lax.dynamic_slice_in_dim(group, mp * region, region, 1)
    own_columns = jnp.where(live_own[:, None], own_columns, jnp.zeros((), jnp.bfloat16))
    strips = block_grams(own_columns, blk).reshape(n_dp, -1, blk)
    height = strips.shape[1]
    count_row = jnp.broadcast_to(counts[0].astype(jnp.float32), (n_dp, 1, blk))
    strips = jnp.concatenate([strips, count_row], axis=1)
    here, there = pair_strips(strips, owner_map)
    there = swap(there, "xl")

    b2, there, other_first, other_second = lax.optimization_barrier(
        (b2, there, other_first, other_second)
    )
    b3 = both_ways(b2, "z", NZ)
    summed = scatter_slots(here + there)
    same = join(other_first, other_second, xh, 0)
    other = join(same, swap(same, "c"), c, 1).reshape(tok_dev, feat)
    grad_theirs = lax.dynamic_slice_in_dim(grad_hidden, (1 - xl) * step, width, 1)
    grad_got = swap(after(grad_theirs, b2), "xl")

    b3, summed = lax.optimization_barrier((b3, summed))
    b4 = both_ways(halves(b3), "z", NZ)
    y2 = both_ways(halves(y1), "y", NY)
    part_b = jnp.zeros((NZ,) + inner.shape, inner.dtype)
    part_b = place(
        part_b,
        [(z, inner), (z + NZ - 1, b1[0]), (z + 1, b1[1]), (z + NZ - 2, b2[0]), (z + 2, b2[1])]
        + [(z + NZ - 3, b3[0]), (z + 3, b3[1]), (z + 4, jnp.concatenate(b4, axis=0))],
        0,
    )
    part_a = jnp.zeros((NZ, NY) + a0.shape, a0.dtype)
    part_a = place(
        part_a,
        [(y, outer), (y + NY - 1, y1[0]), (y + 1, y1[1]), (y + 2, jnp.concatenate(y2, axis=0))],
        1,
    )
    weight_a = part_a.reshape(feat, cut)
    weight_b = part_b.reshape(feat, width - cut)
    input_stat = summed[:height] / summed[height:]
    input_ema = EMA_DECAY * input_factor + (1.0 - EMA_DECAY) * input_stat[None]

    rows = jnp.concatenate([group, other], axis=0)

    def gate(weight):
        sums = jnp.dot(rows, weight, preferred_element_type=jnp.float32)
        return jnp.where(live[:, None], jax.nn.silu(sums), 0.0).astype(jnp.bfloat16)

    grad_mine = lax.dynamic_slice_in_dim(grad_hidden, xl * step, width, 1)
    pick_own = (sampled[:, None] == slot[None, :]).astype(jnp.bfloat16)
    pick_other = (scalars[1:, None] == slot[None, :]).astype(jnp.bfloat16)

    def grams(act, lo, hi):
        own = jnp.dot(pick_own, act[:tok_dev], preferred_element_type=jnp.float32)
        other = jnp.dot(pick_other, act[tok_dev:], preferred_element_type=jnp.float32)
        own = (grad_mine[:, lo:hi].astype(jnp.float32) * own).astype(jnp.bfloat16)
        other = (grad_got[:, lo:hi].astype(jnp.float32) * other).astype(jnp.bfloat16)
        return block_grams(jnp.concatenate([own, other], axis=0), blk)

    act_a = gate(weight_a)
    grams_a = grams(act_a, 0, cut)
    act_b = gate(after(weight_b, grams_a))
    grams_b = grams(act_b, cut, width)
    act = jnp.concatenate([act_a, act_b], axis=1)
    gram = jnp.concatenate([grams_a, grams_b], axis=0)

    away = lax.dynamic_slice_in_dim(act[tok_dev:], xl * (width - step), step, 1)
    back = swap(away, "xl")
    activation = jnp.where(
        xl == 0,
        jnp.concatenate([act[:tok_dev], back], axis=1),
        jnp.concatenate([back, act[:tok_dev]], axis=1),
    )

    n_rest = panel // blk - half_blocks
    gram = jnp.where(
        xl == 0,
        jnp.concatenate([gram, jnp.zeros((n_rest, blk, blk), jnp.float32)], axis=0),
        jnp.concatenate([jnp.zeros((half_blocks, blk, blk), jnp.float32), gram[-n_rest:]], axis=0),
    )
    strips = gram.astype(jnp.bfloat16).reshape(n_dp, -1, blk)
    here, there = pair_strips(strips, owner_map)
    grad_stat = scatter_slots(here + swap(there, "xl"))
    sample_total = jnp.float32(grad_hidden.shape[0] * n_dp)
    grad_ema = EMA_DECAY * grad_factor + (1.0 - EMA_DECAY) * (grad_stat / sample_total)[None]
    return (activation, input_ema, grad_ema)


def solution(mesh):
    fine = Mesh(mesh.devices.reshape(NZ, NY, 2, 2, 2), ("z", "y", "xl", "xh", "c"))
    in_specs = (
        P(DP + MP, None),
        P(DP, MP),
        P(DP, MP),
        P(DP),
        P(DP),
        P(),
        P(MP, DP, None),
        P(MP, DP, None),
    )
    out_specs = (P(DP, MP), P(MP, DP, None), P(MP, DP, None))
    return jax.shard_map(local, mesh=fine, in_specs=in_specs, out_specs=out_specs, check_vma=False)
```

```python
import jax
import jax.numpy as jnp
from jax import lax
from jax.sharding import Mesh, PartitionSpec as P

EMA_DECAY = 0.8
NZ, NY = 8, 4
DP = ("z", "y", "xl")
MP = ("xh", "c")


def swap(x, axis):
    return lax.ppermute(x, axis, [(0, 1), (1, 0)])


def after(x, earlier):
    return lax.optimization_barrier((x, earlier))[0]


def shift(x, axis, n, by):
    return lax.ppermute(x, axis, [(i, (i + by) % n) for i in range(n)])


def put(buf, piece, index, dim):
    return lax.dynamic_update_slice_in_dim(buf, jnp.expand_dims(piece, dim), index, dim)


def ring_gather(x, axis, n, dim, late=None):
    me = lax.axis_index(axis)
    shape = x.shape[:dim] + (n,) + x.shape[dim:]
    buf = put(jnp.zeros(shape, x.dtype), x, me, dim)
    half = x.shape[0] // 2
    up, down = x, x
    for k in range(1, n // 2):
        up, down = shift(up, axis, n, 1), shift(down, axis, n, -1)
        buf = put(buf, up, lax.rem(me - k + n, n), dim)
        buf = put(buf, down, lax.rem(me + k, n), dim)
    up, down = up[:half], down[half:]
    if late is not None:
        up, down = after((up, down), late)
    last = jnp.concatenate([shift(up, axis, n, 1), shift(down, axis, n, -1)], axis=0)
    return put(buf, last, lax.rem(me + n // 2, n), dim)


def direct_gather(x, axis, n):
    me = lax.axis_index(axis)
    buf = put(jnp.zeros((n,) + x.shape, x.dtype), x, me, 0)
    for k in range(1, n):
        buf = put(buf, shift(x, axis, n, k), lax.rem(me - k + n, n), 0)
    return buf


def block_grams(rows, blk):
    stacked = rows.reshape(rows.shape[0], -1, blk)
    return jnp.einsum("tkb,tkc->kbc", stacked, stacked, preferred_element_type=jnp.float32)


def pair_strips(strips, owner_map):
    xl = lax.axis_index("xl")
    slots = jnp.take(strips, owner_map, axis=0, mode="clip")
    slots = slots.reshape((NZ * NY, 2) + strips.shape[1:])
    here = lax.dynamic_index_in_dim(slots, xl, 1, keepdims=False)
    there = lax.dynamic_index_in_dim(slots, 1 - xl, 1, keepdims=False)
    return here, there


def scatter_slots(slots):
    got = lax.all_to_all(slots, ("z", "y"), 0, 0, tiled=False)
    return jnp.sum(got.astype(jnp.float32), axis=0)


def local(tokens, gate_weight, grad_hidden, counts, sampled, owner_map, input_factor, grad_factor):
    blk = input_factor.shape[2]
    n_dp = owner_map.shape[0]
    feat = tokens.shape[1]
    xl = lax.axis_index("xl")
    c = lax.axis_index("c")
    mp = lax.axis_index("xh") * 2 + c
    panel = gate_weight.shape[1]
    half_blocks = (panel // blk + 1) // 2
    width = half_blocks * blk
    step = panel - width
    cut = (half_blocks + 1) // 2 * blk
    mine = lax.dynamic_slice_in_dim(gate_weight, xl * step, width, 1)
    theirs = lax.dynamic_slice_in_dim(gate_weight, (1 - xl) * step, width, 1)
    got = swap(theirs, "xl")
    shard = jnp.where(
        xl == 0, jnp.concatenate([mine, got], axis=0), jnp.concatenate([got, mine], axis=0)
    )
    tok_dev = 4 * tokens.shape[0]
    slot = lax.iota(jnp.int32, tok_dev)
    scalars = swap(jnp.concatenate([counts, sampled]), "xl")
    group = lax.all_gather(after(tokens, got), MP, axis=0, tiled=True)
    live_own = slot < counts[0]
    live_other = slot < scalars[0]
    live = jnp.concatenate([live_own, live_other])

    region = feat // 4
    own_columns = lax.dynamic_slice_in_dim(group, mp * region, region, 1)
    own_columns = jnp.where(live_own[:, None], own_columns, jnp.zeros((), jnp.bfloat16))
    strips = block_grams(own_columns, blk).reshape(n_dp, -1, blk)
    height = strips.shape[1]
    count_row = jnp.broadcast_to(counts[0].astype(jnp.float32), (n_dp, 1, blk))
    strips = jnp.concatenate([strips, count_row], axis=1)
    here, there = pair_strips(strips, owner_map)
    there = swap(there, "xl")
    summed = scatter_slots(here + there)
    input_stat = summed[:height] / summed[height:]
    input_ema = EMA_DECAY * input_factor + (1.0 - EMA_DECAY) * input_stat[None]

    quarter = tok_dev // 4
    late_group = after(group, there)
    near = lax.dynamic_slice_in_dim(late_group, c * 2 * quarter, quarter, 0)
    far = lax.dynamic_slice_in_dim(late_group, c * 2 * quarter + quarter, quarter, 0)
    near = swap(near, "xl")
    far = lax.ppermute(far, ("xl", "xh"), [(0, 3), (1, 2), (2, 1), (3, 0)])
    mine = jnp.concatenate([near, far], axis=0)
    rest = swap(mine, "c")
    other = jnp.where(
        c == 0, jnp.concatenate([mine, rest], axis=0), jnp.concatenate([rest, mine], axis=0)
    )

    part_a = ring_gather(shard[:, :cut], "z", NZ, 0)
    part_a = ring_gather(part_a, "y", NY, 1)
    part_b = direct_gather(shard[:, cut:], "y", NY)
    part_b = ring_gather(part_b.reshape(-1, width - cut), "z", NZ, 0, summed)
    weight_a = part_a.reshape(feat, cut)
    weight_b = part_b.reshape(feat, width - cut)
    grad_theirs = lax.dynamic_slice_in_dim(grad_hidden, (1 - xl) * step, width, 1)
    grad_got = swap(after(grad_theirs, near), "xl")

    rows = jnp.concatenate([group, other], axis=0)

    def gate(weight):
        sums = jnp.dot(rows, weight, preferred_element_type=jnp.float32)
        return jnp.where(live[:, None], jax.nn.silu(sums), 0.0).astype(jnp.bfloat16)

    grad_mine = lax.dynamic_slice_in_dim(grad_hidden, xl * step, width, 1)
    pick_own = (sampled[:, None] == slot[None, :]).astype(jnp.bfloat16)
    pick_other = (scalars[1:, None] == slot[None, :]).astype(jnp.bfloat16)

    def grams(act, lo, hi):
        own = jnp.dot(pick_own, act[:tok_dev], preferred_element_type=jnp.float32)
        other = jnp.dot(pick_other, act[tok_dev:], preferred_element_type=jnp.float32)
        own = (grad_mine[:, lo:hi].astype(jnp.float32) * own).astype(jnp.bfloat16)
        other = (grad_got[:, lo:hi].astype(jnp.float32) * other).astype(jnp.bfloat16)
        return block_grams(jnp.concatenate([own, other], axis=0), blk)

    act_b = gate(weight_b)
    grams_b = grams(act_b, cut, width)
    act_a = gate(after(weight_a, grams_b))
    grams_a = grams(act_a, 0, cut)
    act = jnp.concatenate([act_a, act_b], axis=1)
    gram = jnp.concatenate([grams_a, grams_b], axis=0)

    away = lax.dynamic_slice_in_dim(act[tok_dev:], xl * (width - step), step, 1)
    back = swap(away, "xl")
    activation = jnp.where(
        xl == 0,
        jnp.concatenate([act[:tok_dev], back], axis=1),
        jnp.concatenate([back, act[:tok_dev]], axis=1),
    )

    n_rest = panel // blk - half_blocks
    gram = jnp.where(
        xl == 0,
        jnp.concatenate([gram, jnp.zeros((n_rest, blk, blk), jnp.float32)], axis=0),
        jnp.concatenate([jnp.zeros((half_blocks, blk, blk), jnp.float32), gram[-n_rest:]], axis=0),
    )
    strips = gram.astype(jnp.bfloat16).reshape(n_dp, -1, blk)
    here, there = pair_strips(strips, owner_map)
    grad_stat = scatter_slots(here + swap(there, "xl"))
    sample_total = jnp.float32(grad_hidden.shape[0] * n_dp)
    grad_ema = EMA_DECAY * grad_factor + (1.0 - EMA_DECAY) * (grad_stat / sample_total)[None]
    return (activation, input_ema, grad_ema)


def solution(mesh):
    fine = Mesh(mesh.devices.reshape(NZ, NY, 2, 2, 2), ("z", "y", "xl", "xh", "c"))
    in_specs = (
        P(DP + MP, None),
        P(DP, MP),
        P(DP, MP),
        P(DP),
        P(DP),
        P(),
        P(MP, DP, None),
        P(MP, DP, None),
    )
    out_specs = (P(DP, MP), P(MP, DP, None), P(MP, DP, None))
    return jax.shard_map(local, mesh=fine, in_specs=in_specs, out_specs=out_specs, check_vma=False)
```

```python
import jax
import jax.numpy as jnp
from jax import lax
from jax.sharding import Mesh, PartitionSpec as P

EMA_DECAY = 0.8
NZ, NY = 8, 4
DP = ("z", "y", "xl")
MP = ("xh", "c")


def swap(x, axis):
    return lax.ppermute(x, axis, [(0, 1), (1, 0)])


def after(x, earlier):
    return lax.optimization_barrier((x, earlier))[0]


def shift(x, axis, n, by):
    return lax.ppermute(x, axis, [(i, (i + by) % n) for i in range(n)])


def put(buf, piece, index, dim):
    return lax.dynamic_update_slice_in_dim(buf, jnp.expand_dims(piece, dim), index, dim)


def both_ways(pair, axis, n):
    return shift(pair[0], axis, n, 1), shift(pair[1], axis, n, -1)


def halves(pair):
    rows = pair[0].shape[0] // 2
    return pair[0][:rows], pair[1][rows:]


def block_grams(rows, blk):
    stacked = rows.reshape(rows.shape[0], -1, blk)
    return jnp.einsum("tkb,tkc->kbc", stacked, stacked, preferred_element_type=jnp.float32)


def pair_strips(strips, owner_map):
    xl = lax.axis_index("xl")
    slots = jnp.take(strips, owner_map, axis=0, mode="clip")
    slots = slots.reshape((NZ * NY, 2) + strips.shape[1:])
    here = lax.dynamic_index_in_dim(slots, xl, 1, keepdims=False)
    there = lax.dynamic_index_in_dim(slots, 1 - xl, 1, keepdims=False)
    return here, there


def scatter_slots(slots):
    got = lax.all_to_all(slots, ("z", "y"), 0, 0, tiled=False)
    return jnp.sum(got.astype(jnp.float32), axis=0)


def local(tokens, gate_weight, grad_hidden, counts, sampled, owner_map, input_factor, grad_factor):
    blk = input_factor.shape[2]
    n_dp = owner_map.shape[0]
    feat = tokens.shape[1]
    xl = lax.axis_index("xl")
    xh = lax.axis_index("xh")
    c = lax.axis_index("c")
    mp = xh * 2 + c
    panel = gate_weight.shape[1]
    half_blocks = (panel // blk + 1) // 2
    width = half_blocks * blk
    step = panel - width
    cut = (half_blocks + 1) // 2 * blk
    z, y = lax.axis_index("z"), lax.axis_index("y")
    mine = lax.dynamic_slice_in_dim(gate_weight, xl * step, width, 1)
    theirs = lax.dynamic_slice_in_dim(gate_weight, (1 - xl) * step, width, 1)
    got = swap(theirs, "xl")
    shard = jnp.where(
        xl == 0, jnp.concatenate([mine, got], axis=0), jnp.concatenate([got, mine], axis=0)
    )
    def join(first, second, index, dim):
        return jnp.where(
            index == 0, jnp.stack([first, second], axis=dim), jnp.stack([second, first], axis=dim)
        )

    tok_dev = 4 * tokens.shape[0]
    slot = lax.iota(jnp.int32, tok_dev)
    scalars = swap(jnp.concatenate([counts, sampled]), "xl")
    same = join(tokens, swap(after(tokens, got), "xh"), xh, 0)
    group = join(same, swap(same, "c"), c, 1).reshape(tok_dev, feat)
    live_own = slot < counts[0]
    live_other = slot < scalars[0]
    live = jnp.concatenate([live_own, live_other])

    region = feat // 4
    own_columns = lax.dynamic_slice_in_dim(group, mp * region, region, 1)
    own_columns = jnp.where(live_own[:, None], own_columns, jnp.zeros((), jnp.bfloat16))
    strips = block_grams(own_columns, blk).reshape(n_dp, -1, blk)
    height = strips.shape[1]
    count_row = jnp.broadcast_to(counts[0].astype(jnp.float32), (n_dp, 1, blk))
    strips = jnp.concatenate([strips, count_row], axis=1)
    here, there = pair_strips(strips, owner_map)
    there = swap(there, "xl")
    summed = scatter_slots(here + there)
    input_stat = summed[:height] / summed[height:]
    input_ema = EMA_DECAY * input_factor + (1.0 - EMA_DECAY) * input_stat[None]

    late_tokens = after(tokens, there)
    near = swap(late_tokens, "xl")
    far = lax.ppermute(late_tokens, ("xl", "xh"), [(0, 3), (1, 2), (2, 1), (3, 0)])
    same = join(near, far, xh, 0)
    other = join(same, swap(same, "c"), c, 1).reshape(tok_dev, feat)
    grad_theirs = lax.dynamic_slice_in_dim(grad_hidden, (1 - xl) * step, width, 1)
    grad_got = swap(after(grad_theirs, near), "xl")

    def along_y(blocks, first_after, last_after):
        one = jnp.stack(blocks)
        side = both_ways(after((one, one), first_after), "y", NY)
        back = [side[0], side[1]]
        low = [p.reshape(-1, p.shape[-1]) for p in back]
        far_pair = both_ways(after(halves(low), last_after), "y", NY)
        opposite = jnp.concatenate(far_pair, axis=0).reshape(one.shape)
        buf = jnp.zeros((len(blocks), NY) + blocks[0].shape, one.dtype)
        for off, piece in ((0, one), (NY - 1, back[0]), (1, back[1]), (2, opposite)):
            buf = put(buf, piece, lax.rem(y + off, NY), 1)
        return buf.reshape(len(blocks), -1, blocks[0].shape[-1])

    a0, b0 = shard[:, :cut], shard[:, cut:]
    a1 = both_ways((a0, a0), "z", NZ)
    near_a = along_y([a1[0], a0, a1[1]], a1, a1)
    a2 = both_ways(a1, "z", NZ)
    a3 = both_ways(a2, "z", NZ)

    inner = put(jnp.zeros((NY,) + b0.shape, b0.dtype), b0, y, 0)
    for k in range(1, NY):
        inner = put(inner, shift(b0, "y", NY, k), lax.rem(y - k + NY, NY), 0)
    inner = inner.reshape(-1, b0.shape[1])
    b1 = both_ways((inner, inner), "z", NZ)
    a4 = jnp.concatenate(both_ways(after(halves(a3), b1), "z", NZ), axis=0)
    b2 = both_ways(b1, "z", NZ)
    b3 = both_ways(after(b2, there), "z", NZ)
    far_a = along_y([a3[0], a2[0], a2[1], a3[1], a4], near_a, (summed, b3))
    b4 = jnp.concatenate(both_ways(halves(b3), "z", NZ), axis=0)

    rows = jnp.concatenate([group, other], axis=0)
    depth = feat // NZ
    turn = lax.rem(z + NZ - 3, NZ) * depth
    rows = lax.dynamic_slice_in_dim(jnp.concatenate([rows, rows], axis=1), turn, feat, 1)

    def product(first, last, weight):
        part = rows[:, (first + 3) * depth : (last + 4) * depth]
        return jnp.dot(part, weight.reshape(part.shape[1], -1), preferred_element_type=jnp.float32)


    def gate(sums):
        return jnp.where(live[:, None], jax.nn.silu(sums), 0.0).astype(jnp.bfloat16)

    grad_mine = lax.dynamic_slice_in_dim(grad_hidden, xl * step, width, 1)
    pick_own = (sampled[:, None] == slot[None, :]).astype(jnp.bfloat16)
    pick_other = (scalars[1:, None] == slot[None, :]).astype(jnp.bfloat16)

    def grams(act, lo, hi):
        own = jnp.dot(pick_own, act[:tok_dev], preferred_element_type=jnp.float32)
        other = jnp.dot(pick_other, act[tok_dev:], preferred_element_type=jnp.float32)
        own = (grad_mine[:, lo:hi].astype(jnp.float32) * own).astype(jnp.bfloat16)
        other = (grad_got[:, lo:hi].astype(jnp.float32) * other).astype(jnp.bfloat16)
        return block_grams(jnp.concatenate([own, other], axis=0), blk)

    sums_b = product(0, 0, inner)
    for at, block in (
        (-1, b1[0]), (1, b1[1]), (-2, b2[0]), (2, b2[1]), (-3, b3[0]), (3, b3[1])):
        sums_b = sums_b + product(at, at, block)
    act_b = gate(sums_b + product(4, 4, b4))
    grams_b = grams(act_b, cut, width)
    sums_a = product(-1, 1, near_a)
    far_a = after(far_a, grams_b)
    act_a = gate(sums_a + product(-3, -2, far_a[:2]) + product(2, 4, far_a[2:]))
    grams_a = grams(act_a, 0, cut)
    act = jnp.concatenate([act_a, act_b], axis=1)
    gram = jnp.concatenate([grams_a, grams_b], axis=0)

    away = lax.dynamic_slice_in_dim(act[tok_dev:], xl * (width - step), step, 1)
    back = swap(away, "xl")
    activation = jnp.where(
        xl == 0,
        jnp.concatenate([act[:tok_dev], back], axis=1),
        jnp.concatenate([back, act[:tok_dev]], axis=1),
    )

    n_rest = panel // blk - half_blocks
    gram = jnp.where(
        xl == 0,
        jnp.concatenate([gram, jnp.zeros((n_rest, blk, blk), jnp.float32)], axis=0),
        jnp.concatenate([jnp.zeros((half_blocks, blk, blk), jnp.float32), gram[-n_rest:]], axis=0),
    )
    strips = gram.astype(jnp.bfloat16).reshape(n_dp, -1, blk)
    here, there = pair_strips(strips, owner_map)
    grad_stat = scatter_slots(here + swap(there, "xl"))
    sample_total = jnp.float32(grad_hidden.shape[0] * n_dp)
    grad_ema = EMA_DECAY * grad_factor + (1.0 - EMA_DECAY) * (grad_stat / sample_total)[None]
    return (activation, input_ema, grad_ema)


def solution(mesh):
    fine = Mesh(mesh.devices.reshape(NZ, NY, 2, 2, 2), ("z", "y", "xl", "xh", "c"))
    in_specs = (
        P(DP + MP, None),
        P(DP, MP),
        P(DP, MP),
        P(DP),
        P(DP),
        P(),
        P(MP, DP, None),
        P(MP, DP, None),
    )
    out_specs = (P(DP, MP), P(MP, DP, None), P(MP, DP, None))
    return jax.shard_map(local, mesh=fine, in_specs=in_specs, out_specs=out_specs, check_vma=False)
```

```python
import jax
import jax.numpy as jnp
from jax import lax
from jax.sharding import Mesh, PartitionSpec as P

EMA_DECAY = 0.8
NZ, NY = 8, 4
DP = ("z", "y", "xl")
MP = ("xh", "c")


def swap(x, axis):
    return lax.ppermute(x, axis, [(0, 1), (1, 0)])


def after(x, earlier):
    return lax.optimization_barrier((x, earlier))[0]


def shift(x, axis, n, by):
    return lax.ppermute(x, axis, [(i, (i + by) % n) for i in range(n)])


def put(buf, piece, index, dim):
    return lax.dynamic_update_slice_in_dim(buf, jnp.expand_dims(piece, dim), index, dim)


def ring_gather(x, axis, n, dim, late=None):
    me = lax.axis_index(axis)
    shape = x.shape[:dim] + (n,) + x.shape[dim:]
    buf = put(jnp.zeros(shape, x.dtype), x, me, dim)
    half = x.shape[0] // 2
    up, down = x, x
    for k in range(1, n // 2):
        up, down = shift(up, axis, n, 1), shift(down, axis, n, -1)
        buf = put(buf, up, lax.rem(me - k + n, n), dim)
        buf = put(buf, down, lax.rem(me + k, n), dim)
    up, down = up[:half], down[half:]
    if late is not None:
        up, down = after((up, down), late)
    last = jnp.concatenate([shift(up, axis, n, 1), shift(down, axis, n, -1)], axis=0)
    return put(buf, last, lax.rem(me + n // 2, n), dim)


def block_grams(rows, blk):
    stacked = rows.reshape(rows.shape[0], -1, blk)
    return jnp.einsum("tkb,tkc->kbc", stacked, stacked, preferred_element_type=jnp.float32)


def pair_strips(strips, owner_map):
    xl = lax.axis_index("xl")
    slots = jnp.take(strips, owner_map, axis=0, mode="clip")
    slots = slots.reshape((NZ * NY, 2) + strips.shape[1:])
    here = lax.dynamic_index_in_dim(slots, xl, 1, keepdims=False)
    there = lax.dynamic_index_in_dim(slots, 1 - xl, 1, keepdims=False)
    return here, swap(there, "xl")


def scatter_slots(slots):
    got = lax.all_to_all(slots, ("z", "y"), 0, 0, tiled=False)
    return jnp.sum(got.astype(jnp.float32), axis=0)


def local(tokens, gate_weight, grad_hidden, counts, sampled, owner_map, input_factor, grad_factor):
    blk = input_factor.shape[2]
    n_dp = owner_map.shape[0]
    feat = tokens.shape[1]
    xl = lax.axis_index("xl")
    xh = lax.axis_index("xh")
    c = lax.axis_index("c")
    mp = xh * 2 + c
    panel = gate_weight.shape[1]
    half_blocks = (panel // blk + 1) // 2
    width = half_blocks * blk
    step = panel - width
    cut = (half_blocks + 1) // 2 * blk

    mine = lax.dynamic_slice_in_dim(gate_weight, xl * step, width, 1)
    theirs = lax.dynamic_slice_in_dim(gate_weight, (1 - xl) * step, width, 1)
    got = swap(theirs, "xl")
    shard = jnp.where(
        xl == 0, jnp.concatenate([mine, got], axis=0), jnp.concatenate([got, mine], axis=0)
    )
    late_tokens = after(tokens, got)
    from_xh = swap(late_tokens, "xh")
    from_xl = swap(late_tokens, "xl")
    from_both = lax.ppermute(late_tokens, ("xl", "xh"), [(0, 3), (1, 2), (2, 1), (3, 0)])
    same = jnp.where(
        xh == 0,
        jnp.stack([tokens, from_xh, from_xl, from_both]),
        jnp.stack([from_xh, tokens, from_both, from_xl]),
    )
    cross = swap(same, "c")
    rows = jnp.where(c == 0, jnp.stack([same, cross], axis=1), jnp.stack([cross, same], axis=1))
    tok_dev = rows.shape[2] * 4
    rows = rows.reshape(2, tok_dev, feat)
    group = rows[0]

    scalars = jnp.concatenate([counts, sampled])
    other_scalars = swap(scalars, "xl")
    slot = lax.iota(jnp.int32, tok_dev)
    live_own = slot < counts[0]
    live_other = slot < other_scalars[0]
    live = jnp.concatenate([live_own, live_other])

    region = feat // 4
    own_columns = lax.dynamic_slice_in_dim(group, mp * region, region, 1)
    own_columns = jnp.where(live_own[:, None], own_columns, jnp.zeros((), jnp.bfloat16))
    strips = block_grams(own_columns, blk).reshape(n_dp, -1, blk)
    height = strips.shape[1]
    count_row = jnp.broadcast_to(counts[0].astype(jnp.float32), (n_dp, 1, blk))
    here, neighbour = pair_strips(jnp.concatenate([strips, count_row], axis=1), owner_map)
    summed = scatter_slots(here + neighbour)
    rows = after(rows, summed)
    input_stat = summed[:height] / summed[height:]
    input_ema = EMA_DECAY * input_factor + (1.0 - EMA_DECAY) * input_stat[None]

    part_a = ring_gather(shard[:, :cut], "z", NZ, 0)
    part_a = ring_gather(part_a, "y", NY, 1, neighbour)
    part_b = ring_gather(shard[:, cut:], "y", NY, 0)
    part_b = ring_gather(part_b.reshape(-1, width - cut), "z", NZ, 0)
    weight_a = part_a.reshape(feat, cut)
    weight_b = part_b.reshape(feat, width - cut)

    def gate(weight):
        sums = jnp.dot(rows.reshape(2 * tok_dev, feat), weight, preferred_element_type=jnp.float32)
        return jnp.where(live[:, None], jax.nn.silu(sums), 0.0).astype(jnp.bfloat16)

    grad_mine = lax.dynamic_slice_in_dim(grad_hidden, xl * step, width, 1)
    grad_theirs = lax.dynamic_slice_in_dim(grad_hidden, (1 - xl) * step, width, 1)
    grad_got = swap(after(grad_theirs, from_xl), "xl")
    pick_own = (sampled[:, None] == slot[None, :]).astype(jnp.bfloat16)
    pick_other = (other_scalars[1:, None] == slot[None, :]).astype(jnp.bfloat16)

    def grams(act, lo, hi):
        own = jnp.dot(pick_own, act[:tok_dev], preferred_element_type=jnp.float32)
        other = jnp.dot(pick_other, act[tok_dev:], preferred_element_type=jnp.float32)
        own = (grad_mine[:, lo:hi].astype(jnp.float32) * own).astype(jnp.bfloat16)
        other = (grad_got[:, lo:hi].astype(jnp.float32) * other).astype(jnp.bfloat16)
        return block_grams(jnp.concatenate([own, other], axis=0), blk)

    act_b = gate(weight_b)
    grams_b = grams(act_b, cut, width)
    act_a = gate(weight_a)
    grams_a = grams(act_a, 0, cut)
    act = jnp.concatenate([act_a, act_b], axis=1)
    gram = jnp.concatenate([grams_a, grams_b], axis=0)

    n_rest = panel // blk - half_blocks
    gram = jnp.where(
        xl == 0,
        jnp.concatenate([gram, jnp.zeros((n_rest, blk, blk), jnp.float32)], axis=0),
        jnp.concatenate([jnp.zeros((half_blocks, blk, blk), jnp.float32), gram[-n_rest:]], axis=0),
    )
    strips = gram.astype(jnp.bfloat16).reshape(n_dp, -1, blk)
    grad_here, grad_there = pair_strips(strips, owner_map)
    away = lax.dynamic_slice_in_dim(act[tok_dev:], xl * (width - step), step, 1)
    back = swap(after(away, grad_there), "xl")
    activation = jnp.where(
        xl == 0,
        jnp.concatenate([act[:tok_dev], back], axis=1),
        jnp.concatenate([back, act[:tok_dev]], axis=1),
    )
    grad_stat = scatter_slots(grad_here + grad_there)
    sample_total = jnp.float32(grad_hidden.shape[0] * n_dp)
    grad_ema = EMA_DECAY * grad_factor + (1.0 - EMA_DECAY) * (grad_stat / sample_total)[None]
    return (activation, input_ema, grad_ema)


def solution(mesh):
    fine = Mesh(mesh.devices.reshape(NZ, NY, 2, 2, 2), ("z", "y", "xl", "xh", "c"))
    in_specs = (
        P(DP + MP, None),
        P(DP, MP),
        P(DP, MP),
        P(DP),
        P(DP),
        P(),
        P(MP, DP, None),
        P(MP, DP, None),
    )
    out_specs = (P(DP, MP), P(MP, DP, None), P(MP, DP, None))
    return jax.shard_map(local, mesh=fine, in_specs=in_specs, out_specs=out_specs, check_vma=False)
```

```python
import jax
import jax.numpy as jnp
from jax import lax
from jax.sharding import Mesh, PartitionSpec as P

EMA_DECAY = 0.8
NZ, NY = 8, 4
DP = ("z", "y", "xl")
MP = ("xh", "c")


def swap(x, axis):
    return lax.ppermute(x, axis, [(0, 1), (1, 0)])


def after(x, earlier):
    return lax.optimization_barrier((x, earlier))[0]


def shift(x, axis, n, by):
    return lax.ppermute(x, axis, [(i, (i + by) % n) for i in range(n)])


def put(buf, piece, index, dim):
    return lax.dynamic_update_slice_in_dim(buf, jnp.expand_dims(piece, dim), index, dim)


def ring_gather(x, axis, n, dim, third=None):
    me = lax.axis_index(axis)
    shape = x.shape[:dim] + (n,) + x.shape[dim:]
    buf = put(jnp.zeros(shape, x.dtype), x, me, dim)
    half = x.shape[0] // 2
    up, down = x, x
    for k in range(1, n // 2):
        if k == 3 and third is not None:
            up, down = after((up, down), third)
        up, down = shift(up, axis, n, 1), shift(down, axis, n, -1)
        buf = put(buf, up, lax.rem(me - k + n, n), dim)
        buf = put(buf, down, lax.rem(me + k, n), dim)
    up, down = up[:half], down[half:]
    last = jnp.concatenate([shift(up, axis, n, 1), shift(down, axis, n, -1)], axis=0)
    return put(buf, last, lax.rem(me + n // 2, n), dim)


def block_grams(rows, blk):
    stacked = rows.reshape(rows.shape[0], -1, blk)
    return jnp.einsum("tkb,tkc->kbc", stacked, stacked, preferred_element_type=jnp.float32)


def pair_strips(strips, owner_map):
    xl = lax.axis_index("xl")
    slots = jnp.take(strips, owner_map, axis=0, mode="clip")
    slots = slots.reshape((NZ * NY, 2) + strips.shape[1:])
    here = lax.dynamic_index_in_dim(slots, xl, 1, keepdims=False)
    there = lax.dynamic_index_in_dim(slots, 1 - xl, 1, keepdims=False)
    return here, swap(there, "xl")


def scatter_slots(slots):
    got = lax.all_to_all(slots, ("z", "y"), 0, 0, tiled=False)
    return jnp.sum(got.astype(jnp.float32), axis=0)


def local(tokens, gate_weight, grad_hidden, counts, sampled, owner_map, input_factor, grad_factor):
    blk = input_factor.shape[2]
    n_dp = owner_map.shape[0]
    feat = tokens.shape[1]
    xl = lax.axis_index("xl")
    xh = lax.axis_index("xh")
    c = lax.axis_index("c")
    panel = gate_weight.shape[1]
    half_blocks = (panel // blk + 1) // 2
    width = half_blocks * blk
    step = panel - width
    cut = (half_blocks + 1) // 2 * blk

    mine = lax.dynamic_slice_in_dim(gate_weight, xl * step, width, 1)
    theirs = lax.dynamic_slice_in_dim(gate_weight, (1 - xl) * step, width, 1)
    got = swap(theirs, "xl")
    shard = jnp.where(
        xl == 0, jnp.concatenate([mine, got], axis=0), jnp.concatenate([got, mine], axis=0)
    )
    own_columns = after(tokens, got).reshape(tokens.shape[0], 4, -1).transpose(1, 0, 2)
    own_columns = lax.all_to_all(own_columns, MP, 0, 0, tiled=False)
    own_columns = own_columns.reshape(4 * tokens.shape[0], -1)

    late_tokens = after(tokens, own_columns)
    from_xh = swap(late_tokens, "xh")
    from_xl = swap(late_tokens, "xl")
    from_both = lax.ppermute(late_tokens, ("xl", "xh"), [(0, 3), (1, 2), (2, 1), (3, 0)])
    same = jnp.where(
        xh == 0,
        jnp.stack([tokens, from_xh, from_xl, from_both]),
        jnp.stack([from_xh, tokens, from_both, from_xl]),
    )
    cross = swap(same, "c")
    rows = jnp.where(c == 0, jnp.stack([same, cross], axis=1), jnp.stack([cross, same], axis=1))
    tok_dev = rows.shape[2] * 4
    rows = rows.reshape(2, tok_dev, feat)

    scalars = jnp.concatenate([counts, sampled])
    other_scalars = swap(scalars, "xl")
    slot = lax.iota(jnp.int32, tok_dev)
    live_own = slot < counts[0]
    live_other = slot < other_scalars[0]
    live = jnp.concatenate([live_own, live_other])

    own_columns = jnp.where(live_own[:, None], own_columns, jnp.zeros((), jnp.bfloat16))
    strips = block_grams(own_columns, blk).reshape(n_dp, -1, blk)
    height = strips.shape[1]
    count_row = jnp.broadcast_to(counts[0].astype(jnp.float32), (n_dp, 1, blk))
    here, neighbour = pair_strips(jnp.concatenate([strips, count_row], axis=1), owner_map)
    summed = scatter_slots(here + neighbour)
    input_stat = summed[:height] / summed[height:]
    input_ema = EMA_DECAY * input_factor + (1.0 - EMA_DECAY) * input_stat[None]

    part_a = ring_gather(shard[:, :cut], "z", NZ, 0)
    part_a = ring_gather(part_a, "y", NY, 1)
    part_b = ring_gather(shard[:, cut:], "y", NY, 0)
    part_b = ring_gather(part_b.reshape(-1, width - cut), "z", NZ, 0, summed)
    weight_a = part_a.reshape(feat, cut)
    weight_b = part_b.reshape(feat, width - cut)

    def gate(weight):
        sums = jnp.dot(rows.reshape(2 * tok_dev, feat), weight, preferred_element_type=jnp.float32)
        return jnp.where(live[:, None], jax.nn.silu(sums), 0.0).astype(jnp.bfloat16)

    grad_mine = lax.dynamic_slice_in_dim(grad_hidden, xl * step, width, 1)
    grad_theirs = lax.dynamic_slice_in_dim(grad_hidden, (1 - xl) * step, width, 1)
    grad_got = swap(after(grad_theirs, from_xl), "xl")
    pick_own = (sampled[:, None] == slot[None, :]).astype(jnp.bfloat16)
    pick_other = (other_scalars[1:, None] == slot[None, :]).astype(jnp.bfloat16)

    def grams(act, lo, hi):
        own = jnp.dot(pick_own, act[:tok_dev], preferred_element_type=jnp.float32)
        other = jnp.dot(pick_other, act[tok_dev:], preferred_element_type=jnp.float32)
        own = (grad_mine[:, lo:hi].astype(jnp.float32) * own).astype(jnp.bfloat16)
        other = (grad_got[:, lo:hi].astype(jnp.float32) * other).astype(jnp.bfloat16)
        return block_grams(jnp.concatenate([own, other], axis=0), blk)

    act_b = gate(weight_b)
    grams_b = grams(act_b, cut, width)
    act_a = gate(after(weight_a, grams_b))
    grams_a = grams(act_a, 0, cut)
    act = jnp.concatenate([act_a, act_b], axis=1)
    gram = jnp.concatenate([grams_a, grams_b], axis=0)

    n_rest = panel // blk - half_blocks
    gram = jnp.where(
        xl == 0,
        jnp.concatenate([gram, jnp.zeros((n_rest, blk, blk), jnp.float32)], axis=0),
        jnp.concatenate([jnp.zeros((half_blocks, blk, blk), jnp.float32), gram[-n_rest:]], axis=0),
    )
    strips = gram.astype(jnp.bfloat16).reshape(n_dp, -1, blk)
    grad_here, grad_there = pair_strips(strips, owner_map)
    away = lax.dynamic_slice_in_dim(act[tok_dev:], xl * (width - step), step, 1)
    back = swap(after(away, grad_there), "xl")
    activation = jnp.where(
        xl == 0,
        jnp.concatenate([act[:tok_dev], back], axis=1),
        jnp.concatenate([back, act[:tok_dev]], axis=1),
    )
    grad_stat = scatter_slots(grad_here + grad_there)
    sample_total = jnp.float32(grad_hidden.shape[0] * n_dp)
    grad_ema = EMA_DECAY * grad_factor + (1.0 - EMA_DECAY) * (grad_stat / sample_total)[None]
    return (activation, input_ema, grad_ema)


def solution(mesh):
    fine = Mesh(mesh.devices.reshape(NZ, NY, 2, 2, 2), ("z", "y", "xl", "xh", "c"))
    in_specs = (
        P(DP + MP, None),
        P(DP, MP),
        P(DP, MP),
        P(DP),
        P(DP),
        P(),
        P(MP, DP, None),
        P(MP, DP, None),
    )
    out_specs = (P(DP, MP), P(MP, DP, None), P(MP, DP, None))
    return jax.shard_map(local, mesh=fine, in_specs=in_specs, out_specs=out_specs, check_vma=False)
```

```python
import jax
import jax.numpy as jnp
from jax import lax
from jax.sharding import Mesh, PartitionSpec as P

EMA_DECAY = 0.8
NZ, NY = 8, 4
DP = ("z", "y", "xl")
MP = ("xh", "c")


def swap(x, axis):
    return lax.ppermute(x, axis, [(0, 1), (1, 0)])


def after(x, earlier):
    return lax.optimization_barrier((x, earlier))[0]


def shift(x, axis, n, by):
    return lax.ppermute(x, axis, [(i, (i + by) % n) for i in range(n)])


def put(buf, piece, index, dim):
    return lax.dynamic_update_slice_in_dim(buf, jnp.expand_dims(piece, dim), index, dim)


def ring_gather(x, axis, n, dim, late=None):
    me = lax.axis_index(axis)
    shape = x.shape[:dim] + (n,) + x.shape[dim:]
    buf = put(jnp.zeros(shape, x.dtype), x, me, dim)
    half = x.shape[0] // 2
    up, down = x, x
    for k in range(1, n // 2):
        up, down = shift(up, axis, n, 1), shift(down, axis, n, -1)
        buf = put(buf, up, lax.rem(me - k + n, n), dim)
        buf = put(buf, down, lax.rem(me + k, n), dim)
    up, down = up[:half], down[half:]
    if late is not None:
        up, down = after((up, down), late)
    last = jnp.concatenate([shift(up, axis, n, 1), shift(down, axis, n, -1)], axis=0)
    return put(buf, last, lax.rem(me + n // 2, n), dim)


def block_grams(rows, blk):
    stacked = rows.reshape(rows.shape[0], -1, blk)
    return jnp.einsum("tkb,tkc->kbc", stacked, stacked, preferred_element_type=jnp.float32)


def pair_strips(strips, owner_map):
    xl = lax.axis_index("xl")
    slots = jnp.take(strips, owner_map, axis=0, mode="clip")
    slots = slots.reshape((NZ * NY, 2) + strips.shape[1:])
    here = lax.dynamic_index_in_dim(slots, xl, 1, keepdims=False)
    there = lax.dynamic_index_in_dim(slots, 1 - xl, 1, keepdims=False)
    return here, swap(there, "xl")


def scatter_slots(slots):
    got = lax.all_to_all(slots, ("z", "y"), 0, 0, tiled=False)
    return jnp.sum(got.astype(jnp.float32), axis=0)


def local(tokens, gate_weight, grad_hidden, counts, sampled, owner_map, input_factor, grad_factor):
    blk = input_factor.shape[2]
    n_dp = owner_map.shape[0]
    feat = tokens.shape[1]
    xl = lax.axis_index("xl")
    xh = lax.axis_index("xh")
    c = lax.axis_index("c")
    panel = gate_weight.shape[1]
    half_blocks = (panel // blk + 1) // 2
    width = half_blocks * blk
    step = panel - width
    cut = (half_blocks + 1) // 2 * blk

    mine = lax.dynamic_slice_in_dim(gate_weight, xl * step, width, 1)
    theirs = lax.dynamic_slice_in_dim(gate_weight, (1 - xl) * step, width, 1)
    got = swap(theirs, "xl")
    shard = jnp.where(
        xl == 0, jnp.concatenate([mine, got], axis=0), jnp.concatenate([got, mine], axis=0)
    )
    own_columns = after(tokens, got).reshape(tokens.shape[0], 4, -1).transpose(1, 0, 2)
    own_columns = lax.all_to_all(own_columns, MP, 0, 0, tiled=False)
    own_columns = own_columns.reshape(4 * tokens.shape[0], -1)

    late_tokens = after(tokens, got)
    from_xh = swap(late_tokens, "xh")
    from_xl = swap(late_tokens, "xl")
    from_both = lax.ppermute(late_tokens, ("xl", "xh"), [(0, 3), (1, 2), (2, 1), (3, 0)])
    same = jnp.where(
        xh == 0,
        jnp.stack([tokens, from_xh, from_xl, from_both]),
        jnp.stack([from_xh, tokens, from_both, from_xl]),
    )
    cross = swap(same, "c")
    rows = jnp.where(c == 0, jnp.stack([same, cross], axis=1), jnp.stack([cross, same], axis=1))
    tok_dev = rows.shape[2] * 4
    rows = rows.reshape(2, tok_dev, feat)

    scalars = jnp.concatenate([counts, sampled])
    other_scalars = swap(scalars, "xl")
    slot = lax.iota(jnp.int32, tok_dev)
    live_own = slot < counts[0]
    live_other = slot < other_scalars[0]
    live = jnp.concatenate([live_own, live_other])

    own_columns = jnp.where(live_own[:, None], own_columns, jnp.zeros((), jnp.bfloat16))
    strips = block_grams(own_columns, blk).reshape(n_dp, -1, blk)
    height = strips.shape[1]
    count_row = jnp.broadcast_to(counts[0].astype(jnp.float32), (n_dp, 1, blk))
    here, neighbour = pair_strips(jnp.concatenate([strips, count_row], axis=1), owner_map)
    summed = scatter_slots(here + neighbour)
    input_stat = summed[:height] / summed[height:]
    input_ema = EMA_DECAY * input_factor + (1.0 - EMA_DECAY) * input_stat[None]

    part_a = ring_gather(shard[:, :cut], "z", NZ, 0)
    part_a = ring_gather(part_a, "y", NY, 1)
    part_b = ring_gather(shard[:, cut:], "y", NY, 0)
    part_b = ring_gather(part_b.reshape(-1, width - cut), "z", NZ, 0, summed)
    weight_a = part_a.reshape(feat, cut)
    weight_b = part_b.reshape(feat, width - cut)

    def gate(weight):
        sums = jnp.dot(rows.reshape(2 * tok_dev, feat), weight, preferred_element_type=jnp.float32)
        return jnp.where(live[:, None], jax.nn.silu(sums), 0.0).astype(jnp.bfloat16)

    grad_mine = lax.dynamic_slice_in_dim(grad_hidden, xl * step, width, 1)
    grad_theirs = lax.dynamic_slice_in_dim(grad_hidden, (1 - xl) * step, width, 1)
    grad_got = swap(after(grad_theirs, from_xl), "xl")
    pick_own = (sampled[:, None] == slot[None, :]).astype(jnp.bfloat16)
    pick_other = (other_scalars[1:, None] == slot[None, :]).astype(jnp.bfloat16)

    def grams(act, lo, hi):
        own = jnp.dot(pick_own, act[:tok_dev], preferred_element_type=jnp.float32)
        other = jnp.dot(pick_other, act[tok_dev:], preferred_element_type=jnp.float32)
        own = (grad_mine[:, lo:hi].astype(jnp.float32) * own).astype(jnp.bfloat16)
        other = (grad_got[:, lo:hi].astype(jnp.float32) * other).astype(jnp.bfloat16)
        return block_grams(jnp.concatenate([own, other], axis=0), blk)

    act_b = gate(weight_b)
    grams_b = grams(act_b, cut, width)
    act_a = gate(after(weight_a, grams_b))
    grams_a = grams(act_a, 0, cut)
    act = jnp.concatenate([act_a, act_b], axis=1)
    gram = jnp.concatenate([grams_a, grams_b], axis=0)

    n_rest = panel // blk - half_blocks
    gram = jnp.where(
        xl == 0,
        jnp.concatenate([gram, jnp.zeros((n_rest, blk, blk), jnp.float32)], axis=0),
        jnp.concatenate([jnp.zeros((half_blocks, blk, blk), jnp.float32), gram[-n_rest:]], axis=0),
    )
    strips = gram.astype(jnp.bfloat16).reshape(n_dp, -1, blk)
    grad_here, grad_there = pair_strips(strips, owner_map)
    away = lax.dynamic_slice_in_dim(act[tok_dev:], xl * (width - step), step, 1)
    back = swap(after(away, grad_there), "xl")
    activation = jnp.where(
        xl == 0,
        jnp.concatenate([act[:tok_dev], back], axis=1),
        jnp.concatenate([back, act[:tok_dev]], axis=1),
    )
    grad_stat = scatter_slots(grad_here + grad_there)
    sample_total = jnp.float32(grad_hidden.shape[0] * n_dp)
    grad_ema = EMA_DECAY * grad_factor + (1.0 - EMA_DECAY) * (grad_stat / sample_total)[None]
    return (activation, input_ema, grad_ema)


def solution(mesh):
    fine = Mesh(mesh.devices.reshape(NZ, NY, 2, 2, 2), ("z", "y", "xl", "xh", "c"))
    in_specs = (
        P(DP + MP, None),
        P(DP, MP),
        P(DP, MP),
        P(DP),
        P(DP),
        P(),
        P(MP, DP, None),
        P(MP, DP, None),
    )
    out_specs = (P(DP, MP), P(MP, DP, None), P(MP, DP, None))
    return jax.shard_map(local, mesh=fine, in_specs=in_specs, out_specs=out_specs, check_vma=False)
```

```python
import jax
import jax.numpy as jnp
from jax import lax
from jax.sharding import Mesh, PartitionSpec as P

EMA_DECAY = 0.8
NZ, NY = 8, 4
DP = ("z", "y", "xl")
MP = ("xh", "c")


def swap(x, axis):
    return lax.ppermute(x, axis, [(0, 1), (1, 0)])


def after(x, earlier):
    return lax.optimization_barrier((x, earlier))[0]


def shift(x, axis, n, by):
    return lax.ppermute(x, axis, [(i, (i + by) % n) for i in range(n)])


def put(buf, piece, index, dim):
    return lax.dynamic_update_slice_in_dim(buf, jnp.expand_dims(piece, dim), index, dim)


def ring_blocks(x, axis, n, late=None):
    half = x.shape[0] // 2
    up, down = x, x
    blocks = {0: x}
    for k in range(1, n // 2):
        up, down = shift(up, axis, n, 1), shift(down, axis, n, -1)
        blocks[-k], blocks[k] = up, down
    up, down = up[:half], down[half:]
    if late is not None:
        up, down = after((up, down), late)
    last = jnp.concatenate([shift(up, axis, n, 1), shift(down, axis, n, -1)], axis=0)
    blocks[n // 2] = last
    return blocks


def gather_y(x, dim):
    y = lax.axis_index("y")
    buf = jnp.zeros(x.shape[:dim] + (NY,) + x.shape[dim:], x.dtype)
    blocks = ring_blocks(x, "y", NY)
    for at in blocks:
        buf = put(buf, blocks[at], lax.rem(y + at + NY, NY), dim)
    return buf, blocks[NY // 2]


def block_grams(rows, blk):
    stacked = rows.reshape(rows.shape[0], -1, blk)
    return jnp.einsum("tkb,tkc->kbc", stacked, stacked, preferred_element_type=jnp.float32)


def pair_strips(strips, owner_map):
    xl = lax.axis_index("xl")
    slots = jnp.take(strips, owner_map, axis=0, mode="clip")
    slots = slots.reshape((NZ * NY, 2) + strips.shape[1:])
    here = lax.dynamic_index_in_dim(slots, xl, 1, keepdims=False)
    there = lax.dynamic_index_in_dim(slots, 1 - xl, 1, keepdims=False)
    return here, swap(there, "xl")


def scatter_slots(slots):
    got = lax.all_to_all(slots, ("z", "y"), 0, 0, tiled=False)
    return jnp.sum(got.astype(jnp.float32), axis=0)


def local(tokens, gate_weight, grad_hidden, counts, sampled, owner_map, input_factor, grad_factor):
    blk = input_factor.shape[2]
    n_dp = owner_map.shape[0]
    feat = tokens.shape[1]
    xl = lax.axis_index("xl")
    xh = lax.axis_index("xh")
    c = lax.axis_index("c")
    panel = gate_weight.shape[1]
    half_blocks = (panel // blk + 1) // 2
    width = half_blocks * blk
    step = panel - width
    cut = (half_blocks + 1) // 2 * blk

    mine = lax.dynamic_slice_in_dim(gate_weight, xl * step, width, 1)
    theirs = lax.dynamic_slice_in_dim(gate_weight, (1 - xl) * step, width, 1)
    got = swap(theirs, "xl")
    shard = jnp.where(
        xl == 0, jnp.concatenate([mine, got], axis=0), jnp.concatenate([got, mine], axis=0)
    )
    own_columns = after(tokens, got).reshape(tokens.shape[0], 4, -1).transpose(1, 0, 2)
    own_columns = lax.all_to_all(own_columns, MP, 0, 0, tiled=False)
    own_columns = own_columns.reshape(4 * tokens.shape[0], -1)

    depth = feat // NZ
    z = lax.axis_index("z")
    turned = [
        lax.dynamic_slice_in_dim(tokens, lax.rem(z + NZ + at, NZ) * depth, depth, 1)
        for at in range(1 - NZ // 2, NZ // 2 + 1)
    ]
    tokens = after(jnp.concatenate(turned, axis=1), got)
    from_xh = swap(tokens, "xh")
    from_xl = swap(tokens, "xl")
    from_both = lax.ppermute(tokens, ("xl", "xh"), [(0, 3), (1, 2), (2, 1), (3, 0)])
    same = jnp.where(
        xh == 0,
        jnp.stack([tokens, from_xh, from_xl, from_both]),
        jnp.stack([from_xh, tokens, from_both, from_xl]),
    )
    cross = swap(same, "c")
    rows = jnp.where(c == 0, jnp.stack([same, cross], axis=1), jnp.stack([cross, same], axis=1))
    tok_dev = rows.shape[2] * 4
    rows = rows.reshape(2, tok_dev, feat)

    scalars = jnp.concatenate([counts, sampled])
    other_scalars = swap(scalars, "xl")
    slot = lax.iota(jnp.int32, tok_dev)
    live_own = slot < counts[0]
    live_other = slot < other_scalars[0]
    live = jnp.concatenate([live_own, live_other])

    own_columns = jnp.where(live_own[:, None], own_columns, jnp.zeros((), jnp.bfloat16))
    strips = block_grams(own_columns, blk).reshape(n_dp, -1, blk)
    height = strips.shape[1]
    count_row = jnp.broadcast_to(counts[0].astype(jnp.float32), (n_dp, 1, blk))
    here, neighbour = pair_strips(jnp.concatenate([strips, count_row], axis=1), owner_map)
    summed = scatter_slots(here + neighbour)
    input_stat = summed[:height] / summed[height:]
    input_ema = EMA_DECAY * input_factor + (1.0 - EMA_DECAY) * input_stat[None]

    blocks = ring_blocks(shard[:, :cut], "z", NZ)
    part_a = jnp.stack([blocks[at] for at in sorted(blocks)])
    part_a, last_a = gather_y(part_a, 1)
    part_b, _ = gather_y(shard[:, cut:], 0)
    part_b = ring_blocks(part_b.reshape(-1, width - cut), "z", NZ, (summed, last_a))

    rows = rows.reshape(2 * tok_dev, feat)

    def gate(sums):
        return jnp.where(live[:, None], jax.nn.silu(sums), 0.0).astype(jnp.bfloat16)

    grad_mine = lax.dynamic_slice_in_dim(grad_hidden, xl * step, width, 1)
    grad_theirs = lax.dynamic_slice_in_dim(grad_hidden, (1 - xl) * step, width, 1)
    grad_got = swap(after(grad_theirs, from_xl), "xl")
    pick_own = (sampled[:, None] == slot[None, :]).astype(jnp.bfloat16)
    pick_other = (other_scalars[1:, None] == slot[None, :]).astype(jnp.bfloat16)

    def grams(act, lo, hi):
        own = jnp.dot(pick_own, act[:tok_dev], preferred_element_type=jnp.float32)
        other = jnp.dot(pick_other, act[tok_dev:], preferred_element_type=jnp.float32)
        own = (grad_mine[:, lo:hi].astype(jnp.float32) * own).astype(jnp.bfloat16)
        other = (grad_got[:, lo:hi].astype(jnp.float32) * other).astype(jnp.bfloat16)
        return block_grams(jnp.concatenate([own, other], axis=0), blk)

    act_a = gate(
        jnp.dot(rows, part_a.reshape(feat, cut), preferred_element_type=jnp.float32)
    )
    grams_a = grams(act_a, 0, cut)
    sums = 0.0
    for at in (0, -1, 1, -2, 2, -3, 3, 4):
        first = (at + NZ // 2 - 1) * depth
        sums = sums + jnp.dot(
            rows[:, first : first + depth], part_b[at], preferred_element_type=jnp.float32
        )
    act_b = gate(sums)
    grams_b = grams(act_b, cut, width)
    act = jnp.concatenate([act_a, act_b], axis=1)
    gram = jnp.concatenate([grams_a, grams_b], axis=0)

    n_rest = panel // blk - half_blocks
    gram = jnp.where(
        xl == 0,
        jnp.concatenate([gram, jnp.zeros((n_rest, blk, blk), jnp.float32)], axis=0),
        jnp.concatenate([jnp.zeros((half_blocks, blk, blk), jnp.float32), gram[-n_rest:]], axis=0),
    )
    strips = gram.astype(jnp.bfloat16).reshape(n_dp, -1, blk)
    grad_here, grad_there = pair_strips(strips, owner_map)
    away = lax.dynamic_slice_in_dim(act[tok_dev:], xl * (width - step), step, 1)
    back = swap(after(away, grad_there), "xl")
    activation = jnp.where(
        xl == 0,
        jnp.concatenate([act[:tok_dev], back], axis=1),
        jnp.concatenate([back, act[:tok_dev]], axis=1),
    )
    grad_stat = scatter_slots(grad_here + grad_there)
    sample_total = jnp.float32(grad_hidden.shape[0] * n_dp)
    grad_ema = EMA_DECAY * grad_factor + (1.0 - EMA_DECAY) * (grad_stat / sample_total)[None]
    return (activation, input_ema, grad_ema)


def solution(mesh):
    fine = Mesh(mesh.devices.reshape(NZ, NY, 2, 2, 2), ("z", "y", "xl", "xh", "c"))
    in_specs = (
        P(DP + MP, None),
        P(DP, MP),
        P(DP, MP),
        P(DP),
        P(DP),
        P(),
        P(MP, DP, None),
        P(MP, DP, None),
    )
    out_specs = (P(DP, MP), P(MP, DP, None), P(MP, DP, None))
    return jax.shard_map(local, mesh=fine, in_specs=in_specs, out_specs=out_specs, check_vma=False)
```

```python
import jax
import jax.numpy as jnp
from jax import lax
from jax.sharding import Mesh, PartitionSpec as P

EMA_DECAY = 0.8
NZ, NY = 8, 4
DP = ("z", "y", "xl")
MP = ("xh", "c")


def swap(x, axis):
    return lax.ppermute(x, axis, [(0, 1), (1, 0)])


def after(x, earlier):
    return lax.optimization_barrier((x, earlier))[0]


def shift(x, axis, n, by):
    return lax.ppermute(x, axis, [(i, (i + by) % n) for i in range(n)])


def put(buf, piece, index, dim):
    return lax.dynamic_update_slice_in_dim(buf, jnp.expand_dims(piece, dim), index, dim)


def ring_blocks(x, axis, n, late=None):
    half = x.shape[0] // 2
    up, down = x, x
    blocks = {0: x}
    for k in range(1, n // 2):
        up, down = shift(up, axis, n, 1), shift(down, axis, n, -1)
        blocks[-k], blocks[k] = up, down
    up, down = up[:half], down[half:]
    if late is not None:
        up, down = after((up, down), late)
    last = jnp.concatenate([shift(up, axis, n, 1), shift(down, axis, n, -1)], axis=0)
    blocks[n // 2] = last
    return blocks


def gather_y(x, dim):
    y = lax.axis_index("y")
    buf = jnp.zeros(x.shape[:dim] + (NY,) + x.shape[dim:], x.dtype)
    blocks = ring_blocks(x, "y", NY)
    for at in blocks:
        buf = put(buf, blocks[at], lax.rem(y + at + NY, NY), dim)
    return buf, blocks[NY // 2]


def block_grams(rows, blk):
    stacked = rows.reshape(rows.shape[0], -1, blk)
    return jnp.einsum("tkb,tkc->kbc", stacked, stacked, preferred_element_type=jnp.float32)


def pair_strips(strips, owner_map):
    xl = lax.axis_index("xl")
    slots = jnp.take(strips, owner_map, axis=0, mode="clip")
    slots = slots.reshape((NZ * NY, 2) + strips.shape[1:])
    here = lax.dynamic_index_in_dim(slots, xl, 1, keepdims=False)
    there = lax.dynamic_index_in_dim(slots, 1 - xl, 1, keepdims=False)
    return here, swap(there, "xl")


def scatter_slots(slots):
    got = lax.all_to_all(slots, ("z", "y"), 0, 0, tiled=False)
    return jnp.sum(got.astype(jnp.float32), axis=0)


def local(tokens, gate_weight, grad_hidden, counts, sampled, owner_map, input_factor, grad_factor):
    blk = input_factor.shape[2]
    n_dp = owner_map.shape[0]
    feat = tokens.shape[1]
    xl = lax.axis_index("xl")
    xh = lax.axis_index("xh")
    c = lax.axis_index("c")
    panel = gate_weight.shape[1]
    half_blocks = (panel // blk + 1) // 2
    width = half_blocks * blk
    step = panel - width
    cut = (half_blocks + 1) // 2 * blk

    mine = lax.dynamic_slice_in_dim(gate_weight, xl * step, width, 1)
    theirs = lax.dynamic_slice_in_dim(gate_weight, (1 - xl) * step, width, 1)
    got = swap(theirs, "xl")
    shard = jnp.where(
        xl == 0, jnp.concatenate([mine, got], axis=0), jnp.concatenate([got, mine], axis=0)
    )
    own_columns = after(tokens, got).reshape(tokens.shape[0], 4, -1).transpose(1, 0, 2)
    own_columns = lax.all_to_all(own_columns, MP, 0, 0, tiled=False)
    own_columns = own_columns.reshape(4 * tokens.shape[0], -1)
    live_own = lax.iota(jnp.int32, own_columns.shape[0]) < counts[0]
    own_columns = jnp.where(live_own[:, None], own_columns, jnp.zeros((), jnp.bfloat16))

    depth = feat // NZ
    z = lax.axis_index("z")
    turned = [
        lax.dynamic_slice_in_dim(tokens, lax.rem(z + NZ + at, NZ) * depth, depth, 1)
        for at in range(1 - NZ // 2, NZ // 2 + 1)
    ]
    tokens, own_columns = lax.optimization_barrier((jnp.concatenate(turned, axis=1), own_columns))
    from_xh = swap(tokens, "xh")
    from_xl = swap(tokens, "xl")
    from_both = lax.ppermute(tokens, ("xl", "xh"), [(0, 3), (1, 2), (2, 1), (3, 0)])
    same = jnp.where(
        xh == 0,
        jnp.stack([tokens, from_xh, from_xl, from_both]),
        jnp.stack([from_xh, tokens, from_both, from_xl]),
    )
    cross = swap(same, "c")
    rows = jnp.where(c == 0, jnp.stack([same, cross], axis=1), jnp.stack([cross, same], axis=1))
    tok_dev = rows.shape[2] * 4
    rows = rows.reshape(2, tok_dev, feat)

    scalars = jnp.concatenate([counts, sampled])
    other_scalars = swap(scalars, "xl")
    slot = lax.iota(jnp.int32, tok_dev)
    live_other = slot < other_scalars[0]
    live = jnp.concatenate([live_own, live_other])

    strips = block_grams(own_columns, blk).reshape(n_dp, -1, blk)
    height = strips.shape[1]
    count_row = jnp.broadcast_to(counts[0].astype(jnp.float32), (n_dp, 1, blk))
    here, neighbour = pair_strips(jnp.concatenate([strips, count_row], axis=1), owner_map)
    summed = scatter_slots(here + neighbour)
    input_stat = summed[:height] / summed[height:]
    input_ema = EMA_DECAY * input_factor + (1.0 - EMA_DECAY) * input_stat[None]

    blocks = ring_blocks(shard[:, :cut], "z", NZ)
    part_a = jnp.stack([blocks[at] for at in sorted(blocks)])
    part_a, last_a = gather_y(part_a, 1)
    part_b, _ = gather_y(shard[:, cut:], 0)
    part_b = ring_blocks(part_b.reshape(-1, width - cut), "z", NZ, (summed, last_a))

    rows = rows.reshape(2 * tok_dev, feat)

    def gate(sums):
        return jnp.where(live[:, None], jax.nn.silu(sums), 0.0).astype(jnp.bfloat16)

    grad_mine = lax.dynamic_slice_in_dim(grad_hidden, xl * step, width, 1)
    grad_theirs = lax.dynamic_slice_in_dim(grad_hidden, (1 - xl) * step, width, 1)
    grad_got = swap(after(grad_theirs, from_xl), "xl")
    pick_own = (sampled[:, None] == slot[None, :]).astype(jnp.bfloat16)
    pick_other = (other_scalars[1:, None] == slot[None, :]).astype(jnp.bfloat16)

    def grams(act, lo, hi):
        own = jnp.dot(pick_own, act[:tok_dev], preferred_element_type=jnp.float32)
        other = jnp.dot(pick_other, act[tok_dev:], preferred_element_type=jnp.float32)
        own = (grad_mine[:, lo:hi].astype(jnp.float32) * own).astype(jnp.bfloat16)
        other = (grad_got[:, lo:hi].astype(jnp.float32) * other).astype(jnp.bfloat16)
        return block_grams(jnp.concatenate([own, other], axis=0), blk)

    act_a = gate(
        jnp.dot(rows, part_a.reshape(feat, cut), preferred_element_type=jnp.float32)
    )
    grams_a = grams(act_a, 0, cut)
    sums = 0.0
    for at in (0, -1, 1, -2, 2, -3, 3, 4):
        first = (at + NZ // 2 - 1) * depth
        sums = sums + jnp.dot(
            rows[:, first : first + depth], part_b[at], preferred_element_type=jnp.float32
        )
    act_b = gate(sums)
    grams_b = grams(act_b, cut, width)
    act = jnp.concatenate([act_a, act_b], axis=1)
    gram = jnp.concatenate([grams_a, grams_b], axis=0)

    n_rest = panel // blk - half_blocks
    gram = jnp.where(
        xl == 0,
        jnp.concatenate([gram, jnp.zeros((n_rest, blk, blk), jnp.float32)], axis=0),
        jnp.concatenate([jnp.zeros((half_blocks, blk, blk), jnp.float32), gram[-n_rest:]], axis=0),
    )
    strips = gram.astype(jnp.bfloat16).reshape(n_dp, -1, blk)
    grad_here, grad_there = pair_strips(strips, owner_map)
    away = lax.dynamic_slice_in_dim(act[tok_dev:], xl * (width - step), step, 1)
    back = swap(after(away, grad_there), "xl")
    activation = jnp.where(
        xl == 0,
        jnp.concatenate([act[:tok_dev], back], axis=1),
        jnp.concatenate([back, act[:tok_dev]], axis=1),
    )
    grad_stat = scatter_slots(grad_here + grad_there)
    sample_total = jnp.float32(grad_hidden.shape[0] * n_dp)
    grad_ema = EMA_DECAY * grad_factor + (1.0 - EMA_DECAY) * (grad_stat / sample_total)[None]
    return (activation, input_ema, grad_ema)


def solution(mesh):
    fine = Mesh(mesh.devices.reshape(NZ, NY, 2, 2, 2), ("z", "y", "xl", "xh", "c"))
    in_specs = (
        P(DP + MP, None),
        P(DP, MP),
        P(DP, MP),
        P(DP),
        P(DP),
        P(),
        P(MP, DP, None),
        P(MP, DP, None),
    )
    out_specs = (P(DP, MP), P(MP, DP, None), P(MP, DP, None))
    return jax.shard_map(local, mesh=fine, in_specs=in_specs, out_specs=out_specs, check_vma=False)
```

```python
import jax
import jax.numpy as jnp
from jax import lax
from jax.sharding import Mesh, PartitionSpec as P

EMA_DECAY = 0.8
NZ, NY = 8, 4
DP = ("z", "y", "xl")
MP = ("xh", "c")


def swap(x, axis):
    return lax.ppermute(x, axis, [(0, 1), (1, 0)])


def after(x, earlier):
    return lax.optimization_barrier((x, earlier))[0]


def shift(x, axis, n, by):
    return lax.ppermute(x, axis, [(i, (i + by) % n) for i in range(n)])


def put(buf, piece, index, dim):
    return lax.dynamic_update_slice_in_dim(buf, jnp.expand_dims(piece, dim), index, dim)


def ring_blocks(x, axis, n, late=None):
    half = x.shape[0] // 2
    up, down = x, x
    blocks = {0: x}
    for k in range(1, n // 2):
        up, down = shift(up, axis, n, 1), shift(down, axis, n, -1)
        blocks[-k], blocks[k] = up, down
    up, down = up[:half], down[half:]
    if late is not None:
        up, down = after((up, down), late)
    last = jnp.concatenate([shift(up, axis, n, 1), shift(down, axis, n, -1)], axis=0)
    blocks[n // 2] = last
    return blocks


def gather_y(x, dim):
    y = lax.axis_index("y")
    buf = jnp.zeros(x.shape[:dim] + (NY,) + x.shape[dim:], x.dtype)
    blocks = ring_blocks(x, "y", NY)
    for at in blocks:
        buf = put(buf, blocks[at], lax.rem(y + at + NY, NY), dim)
    return buf, blocks[NY // 2]


def block_grams(rows, blk):
    stacked = rows.reshape(rows.shape[0], -1, blk)
    return jnp.einsum("tkb,tkc->kbc", stacked, stacked, preferred_element_type=jnp.float32)


def pair_strips(strips, owner_map):
    xl = lax.axis_index("xl")
    slots = jnp.take(strips, owner_map, axis=0, mode="clip")
    slots = slots.reshape((NZ * NY, 2) + strips.shape[1:])
    here = lax.dynamic_index_in_dim(slots, xl, 1, keepdims=False)
    there = lax.dynamic_index_in_dim(slots, 1 - xl, 1, keepdims=False)
    return here, swap(there, "xl")


def scatter_slots(slots):
    got = lax.all_to_all(slots, ("z", "y"), 0, 0, tiled=False)
    return jnp.sum(got.astype(jnp.float32), axis=0)


def local(tokens, gate_weight, grad_hidden, counts, sampled, owner_map, input_factor, grad_factor):
    blk = input_factor.shape[2]
    n_dp = owner_map.shape[0]
    feat = tokens.shape[1]
    xl = lax.axis_index("xl")
    xh = lax.axis_index("xh")
    c = lax.axis_index("c")
    panel = gate_weight.shape[1]
    half_blocks = (panel // blk + 1) // 2
    width = half_blocks * blk
    step = panel - width
    cut = (half_blocks + 1) // 2 * blk

    mine = lax.dynamic_slice_in_dim(gate_weight, xl * step, width, 1)
    theirs = lax.dynamic_slice_in_dim(gate_weight, (1 - xl) * step, width, 1)
    got = swap(theirs, "xl")
    shard = jnp.where(
        xl == 0, jnp.concatenate([mine, got], axis=0), jnp.concatenate([got, mine], axis=0)
    )
    own_columns = after(tokens, got).reshape(tokens.shape[0], 4, -1).transpose(1, 0, 2)
    own_columns = lax.all_to_all(own_columns, MP, 0, 0, tiled=False)
    own_columns = own_columns.reshape(4 * tokens.shape[0], -1)
    live_own = lax.iota(jnp.int32, own_columns.shape[0]) < counts[0]
    own_columns = jnp.where(live_own[:, None], own_columns, jnp.zeros((), jnp.bfloat16))

    depth = feat // NZ
    z = lax.axis_index("z")
    turned = [
        lax.dynamic_slice_in_dim(tokens, lax.rem(z + NZ + at, NZ) * depth, depth, 1)
        for at in range(1 - NZ // 2, NZ // 2 + 1)
    ]
    tokens, own_columns = lax.optimization_barrier((jnp.concatenate(turned, axis=1), own_columns))
    from_xh = swap(tokens, "xh")
    from_xl = swap(after(tokens, from_xh), "xl")
    from_both = lax.ppermute(after(tokens, from_xl), ("xl", "xh"), [(0, 3), (1, 2), (2, 1), (3, 0)])
    same = jnp.where(
        xh == 0,
        jnp.stack([tokens, from_xh, from_xl, from_both]),
        jnp.stack([from_xh, tokens, from_both, from_xl]),
    )
    cross = swap(same, "c")
    rows = jnp.where(c == 0, jnp.stack([same, cross], axis=1), jnp.stack([cross, same], axis=1))
    tok_dev = rows.shape[2] * 4
    rows = rows.reshape(2, tok_dev, feat)

    scalars = jnp.concatenate([counts, sampled])
    other_scalars = swap(scalars, "xl")
    slot = lax.iota(jnp.int32, tok_dev)
    live_other = slot < other_scalars[0]
    live = jnp.concatenate([live_own, live_other])

    strips = block_grams(own_columns, blk).reshape(n_dp, -1, blk)
    height = strips.shape[1]
    count_row = jnp.broadcast_to(counts[0].astype(jnp.float32), (n_dp, 1, blk))
    here, neighbour = pair_strips(jnp.concatenate([strips, count_row], axis=1), owner_map)
    summed = scatter_slots(here + neighbour)
    input_stat = summed[:height] / summed[height:]
    input_ema = EMA_DECAY * input_factor + (1.0 - EMA_DECAY) * input_stat[None]

    blocks = ring_blocks(shard[:, :cut], "z", NZ)
    part_a = jnp.stack([blocks[at] for at in sorted(blocks)])
    part_a, last_a = gather_y(part_a, 1)
    part_b, _ = gather_y(shard[:, cut:], 0)
    part_b = ring_blocks(part_b.reshape(-1, width - cut), "z", NZ, (summed, last_a))

    rows = rows.reshape(2 * tok_dev, feat)

    def gate(sums):
        return jnp.where(live[:, None], jax.nn.silu(sums), 0.0).astype(jnp.bfloat16)

    grad_mine = lax.dynamic_slice_in_dim(grad_hidden, xl * step, width, 1)
    grad_theirs = lax.dynamic_slice_in_dim(grad_hidden, (1 - xl) * step, width, 1)
    grad_got = swap(after(grad_theirs, from_xl), "xl")
    pick_own = (sampled[:, None] == slot[None, :]).astype(jnp.bfloat16)
    pick_other = (other_scalars[1:, None] == slot[None, :]).astype(jnp.bfloat16)

    def grams(act, lo, hi):
        own = jnp.dot(pick_own, act[:tok_dev], preferred_element_type=jnp.float32)
        other = jnp.dot(pick_other, act[tok_dev:], preferred_element_type=jnp.float32)
        own = (grad_mine[:, lo:hi].astype(jnp.float32) * own).astype(jnp.bfloat16)
        other = (grad_got[:, lo:hi].astype(jnp.float32) * other).astype(jnp.bfloat16)
        return block_grams(jnp.concatenate([own, other], axis=0), blk)

    act_a = gate(
        jnp.dot(rows, part_a.reshape(feat, cut), preferred_element_type=jnp.float32)
    )
    grams_a = grams(act_a, 0, cut)
    sums = 0.0
    for at in (0, -1, 1, -2, 2, -3, 3, 4):
        first = (at + NZ // 2 - 1) * depth
        sums = sums + jnp.dot(
            rows[:, first : first + depth], part_b[at], preferred_element_type=jnp.float32
        )
    act_b = gate(sums)
    grams_b = grams(act_b, cut, width)
    act = jnp.concatenate([act_a, act_b], axis=1)
    gram = jnp.concatenate([grams_a, grams_b], axis=0)

    n_rest = panel // blk - half_blocks
    gram = jnp.where(
        xl == 0,
        jnp.concatenate([gram, jnp.zeros((n_rest, blk, blk), jnp.float32)], axis=0),
        jnp.concatenate([jnp.zeros((half_blocks, blk, blk), jnp.float32), gram[-n_rest:]], axis=0),
    )
    strips = gram.astype(jnp.bfloat16).reshape(n_dp, -1, blk)
    grad_here, grad_there = pair_strips(strips, owner_map)
    away = lax.dynamic_slice_in_dim(act[tok_dev:], xl * (width - step), step, 1)
    back = swap(after(away, grad_there), "xl")
    activation = jnp.where(
        xl == 0,
        jnp.concatenate([act[:tok_dev], back], axis=1),
        jnp.concatenate([back, act[:tok_dev]], axis=1),
    )
    grad_stat = scatter_slots(grad_here + grad_there)
    sample_total = jnp.float32(grad_hidden.shape[0] * n_dp)
    grad_ema = EMA_DECAY * grad_factor + (1.0 - EMA_DECAY) * (grad_stat / sample_total)[None]
    return (activation, input_ema, grad_ema)


def solution(mesh):
    fine = Mesh(mesh.devices.reshape(NZ, NY, 2, 2, 2), ("z", "y", "xl", "xh", "c"))
    in_specs = (
        P(DP + MP, None),
        P(DP, MP),
        P(DP, MP),
        P(DP),
        P(DP),
        P(),
        P(MP, DP, None),
        P(MP, DP, None),
    )
    out_specs = (P(DP, MP), P(MP, DP, None), P(MP, DP, None))
    return jax.shard_map(local, mesh=fine, in_specs=in_specs, out_specs=out_specs, check_vma=False)
```
